512 devices in a mesh: row: 32 (over x, z), col: 16 (over y, core).
Axes of the slice: x: 4, y: 8, z: 8, core: 2. Of those that a mesh axis runs over, the one named last changes fastest.
Arguments:
- query_nope: bfloat16 [8, 128, 128], P(None, 'row'), may hold values from -9 to 9
- query_rope: bfloat16 [8, 128, 64], P(None, 'row'), may hold values from -10 to 80
- key_up_weight: bfloat16 [128, 128, 512], P('row'), may hold values from -0.5 to 0.5
- value_up_weight: bfloat16 [128, 512, 128], P('row'), may hold values from -0.25 to 0.25
- latent_cache: bfloat16 [2097152, 576], P(('row', 'col')), may hold values from -6 to 6
- lengths: int32 [8], replicated, may hold values from 1 to 262144, as said below
- page_table: int32 [8, 4096], replicated, may hold values from -1 to 32767, as said below
Outputs:
- head_values: bfloat16 [8, 16384], P(None, 'row')
The draws below stay inside these ranges and needn't reach their ends.
Inputs may be any that keep to these rules, and one draw needn't show every extreme that they name: `lengths`: the largest length is exactly 262144. `page_table`: entry (r, p) is -1 exactly when p * 64 >= lengths[r]; all other entries are distinct cache pages, page k lying on the device of index k // 64 along row+col.
All inputs are finite; a program needn't handle non-finite values.
Results may differ from the reference program's by a relative error of at most 0.0094.
Values may be sent and summed in bfloat16 or wider, within the bound.
No kernel may reach another device: no remote copies, remote signals or barrier semaphores. Data moves between devices by JAX's collectives and lax.ppermute only.
A program may use at most 128 MiB of HBM per device.

```python
import jax
import jax.numpy as jnp
from jax import lax

HEAD_COUNT = 128
HEAD_NOPE_WIDTH = 128
ROTARY_WIDTH = 64
LATENT_WIDTH = 512
HEAD_VALUE_WIDTH = 128
PAGE = 64
REQS = 8
SLOTS = 32768
PAGES_MAX = 4096
LMAX = 262144
CACHE_ROWS = 2097152


def paged_layout(key):
    leading_key, second_key, third_key = jax.random.split(key, 3)
    longest = jax.random.randint(leading_key, (), 0, REQS)
    spans = jax.random.randint(second_key, (REQS,), 1, LMAX + 1)
    spans = jnp.where(jnp.arange(REQS) == longest, LMAX, spans).astype(jnp.int32)
    order = jax.random.permutation(third_key, SLOTS).astype(jnp.int32).reshape(REQS, PAGES_MAX)
    live = jnp.arange(PAGES_MAX)[None, :] * PAGE < spans[:, None]
    return (spans, jnp.where(live, order, -1).astype(jnp.int32))


def draw_lengths(key, part):
    return paged_layout(key)[0]


def draw_page_table(key, part):
    return paged_layout(key)[1]


def draw_latent_cache(key, part):
    key = jax.random.fold_in(key, 11)
    leading_key = jax.random.fold_in(key, 0)
    return jax.random.truncated_normal(leading_key, -6.0, 6.0, (CACHE_ROWS, LATENT_WIDTH + ROTARY_WIDTH), jnp.float32).astype(jnp.bfloat16)


def draw_query_rope(key, part):
    key = jax.random.fold_in(key, 23)
    leading_key = jax.random.fold_in(key, 0)
    return (2.3 * jax.random.truncated_normal(leading_key, -4.0, 4.0, (REQS, HEAD_COUNT, ROTARY_WIDTH), jnp.float32)).astype(jnp.bfloat16)


def block_levels(key, extent, pieces, smallest, top_value):
    def one(axis_at, parts):
        steps = jax.random.uniform(jax.random.fold_in(jax.random.fold_in(key, 6), axis_at), (parts,), jnp.float32, smallest / len(pieces), top_value / len(pieces))
        return jnp.repeat(jnp.exp(steps), extent[axis_at] // parts).reshape((-1,) + (1,) * (len(extent) - axis_at - 1))

    factor_of = one(*pieces[0])
    for cut in pieces[1:]:
        factor_of = factor_of * one(*cut)
    return factor_of


def centred(rng, shape, deviation, bound, cuts=(), kind=jnp.bfloat16):
    entries = jax.random.normal(rng, shape, jnp.float32) * deviation
    if len(cuts) > 0:
        entries = block_levels(rng, shape, cuts, -0.22, 0.18) * entries
    return jnp.clip(entries, min=-bound, max=bound).astype(kind)


def setup_inputs(seed: int = 0) -> dict:
    splits = jax.random.split(jax.random.key(seed), 8)
    return {
        "query_nope": centred(splits[0], (REQS, HEAD_COUNT, HEAD_NOPE_WIDTH), 2.3, 9.0, ((1, 32),)),
        "query_rope": draw_query_rope(jax.random.fold_in(splits[7], 71), 0),
        "key_up_weight": centred(splits[2], (HEAD_COUNT, HEAD_NOPE_WIDTH, LATENT_WIDTH), HEAD_NOPE_WIDTH ** -0.5, 0.5, ((0, 32),)),
        "value_up_weight": centred(splits[3], (HEAD_COUNT, LATENT_WIDTH, HEAD_VALUE_WIDTH), LATENT_WIDTH ** -0.5, 0.25, ((0, 32),)),
        "latent_cache": draw_latent_cache(jax.random.fold_in(splits[7], 71), 0),
        "lengths": draw_lengths(jax.random.fold_in(splits[7], 71), 0),
        "page_table": draw_page_table(jax.random.fold_in(splits[7], 71), 0),
    }


MASKED = -1.0e30


def reference(query_nope, query_rope, key_up_weight, value_up_weight, latent_cache, lengths, page_table):
    scale = float(HEAD_NOPE_WIDTH + ROTARY_WIDTH) ** -0.5
    query_latent = jnp.einsum('rhn,hnc->rhc', query_nope.astype(jnp.float32), key_up_weight.astype(jnp.float32)).astype(jnp.bfloat16)
    query = jnp.concatenate([query_latent, query_rope], axis=2)
    width = latent_cache.shape[1]
    pages = latent_cache.reshape(SLOTS, PAGE, width)
    span = PAGES_MAX * PAGE

    def one_request(items):
        request_query, length, table_row = items
        key_rows = pages[jnp.maximum(table_row, 0)].reshape(span, width).astype(jnp.float32)
        position = jnp.arange(span, dtype=jnp.int32)
        live = (position < length) & jnp.repeat(table_row >= 0, PAGE)
        scores = jnp.dot(request_query.astype(jnp.float32), key_rows.T) * scale
        scores = jnp.where(live[None, :], scores, MASKED)
        page_top = jnp.max(scores.reshape(HEAD_COUNT, PAGES_MAX, PAGE), axis=2)
        expo = jnp.where(live[None, :], jnp.exp(scores - jnp.repeat(page_top, PAGE, axis=1)), 0.0)
        expo = lax.optimization_barrier(expo.astype(jnp.bfloat16)).astype(jnp.float32)
        top = jnp.max(page_top, axis=1)
        page_weight = jnp.exp(page_top - top[:, None])
        softmax_weight = (expo.reshape(HEAD_COUNT, PAGES_MAX, PAGE) * page_weight[:, :, None]).reshape(HEAD_COUNT, span)
        denom = jnp.sum(softmax_weight, axis=1)
        weighted_latent_sum = jnp.dot(softmax_weight, key_rows[:, :LATENT_WIDTH], precision=lax.Precision.HIGHEST)
        return (weighted_latent_sum / denom[:, None]).astype(jnp.bfloat16)

    attended = lax.map(one_request, (query, lengths, page_table))
    values = jnp.einsum('rhc,hcv->rhv', attended.astype(jnp.float32), value_up_weight.astype(jnp.float32))
    return values.astype(jnp.bfloat16).reshape(REQS, HEAD_COUNT * HEAD_VALUE_WIDTH)
```

```python
import functools

import jax
import jax.numpy as jnp
from jax import lax
from jax.experimental import pallas as pl
from jax.experimental.pallas import tpu as pltpu
from jax.sharding import PartitionSpec as P

PAGE = 64
LANES = 128
EMPTY = -1e30
ENTRIES = 128
TRASH = 150
PLAN = 512
F32 = jnp.float32
BF16 = jnp.bfloat16
VMEM_LIMIT = 48 * 1024 * 1024


def three_terms(value):
    high = value.astype(BF16)
    rest = value - high.astype(F32)
    middle = rest.astype(BF16)
    low = (rest - middle.astype(F32)).astype(BF16)
    return high, middle, low


def stat_lanes(values, rows):
    lane = lax.broadcasted_iota(jnp.int32, (rows, LANES), 1)
    out = jnp.zeros((rows, LANES), F32)
    for head, value in enumerate(values):
        for at, term in enumerate(three_terms(value)):
            out = jnp.where(lane == 64 * head + at, term.astype(F32), out)
    return out


def read_stat(lanes, head):
    at = 64 * head
    return lanes[..., at : at + 1] + lanes[..., at + 1 : at + 2] + lanes[..., at + 2 : at + 3]


def query_kernel(core_ref, nope_ref, rope_ref, up_ref, out_ref):
    first = 2 * core_ref[0]
    copies = out_ref.shape[0]
    kv = up_ref.shape[2]
    parts, ropes = [], []
    for j in range(2):
        product = jnp.dot(nope_ref[first + j], up_ref[j], preferred_element_type=F32)
        parts.append(product.astype(BF16))
        ropes.append(rope_ref[first + j])
    row = jnp.concatenate(parts + ropes, axis=1)
    for k in range(copies):
        out_ref[k] = row


def plan_kernel(where_ref, length_ref, table_ref, plan_ref, vec, sm, count, fill, sem):
    base, core = where_ref[0], where_ref[1]
    requests, width = table_ref.shape
    page = lax.broadcasted_iota(jnp.int32, (1, width), 1)
    high = lax.broadcasted_iota(jnp.int32, (8, width), 0)
    low = lax.broadcasted_iota(jnp.int32, (16, width), 0)
    total = jnp.zeros((16, 16), F32)
    for r in range(requests):
        slot = table_ref[r : r + 1, :] - base
        live = jnp.clip(length_ref[r] - page * PAGE, 0, PAGE).astype(F32)
        hit = high == (slot >> 4)
        owner = jnp.where(hit, float(r + 1), 0.0)
        rows = jnp.where(hit, live, 0.0)
        left = jnp.concatenate([owner, rows], axis=0).astype(BF16)
        right = jnp.where(low == (slot & 15), 1.0, 0.0).astype(BF16)
        total = total + lax.dot_general(
            left, right, (((1,), (1,)), ((), ())), preferred_element_type=F32
        )
    vec[:, :16] = total.astype(jnp.int32)
    copy = pltpu.make_async_copy(vec, sm, sem)
    copy.start()
    copy.wait()

    def page_of(i, side):
        s = (2 * i + side + PAGE * core) & 127
        return sm[s >> 4, s & 15], sm[8 + (s >> 4), s & 15]

    for r in range(16):
        count[r] = 0

    @pl.loop(0, PLAN)
    def _(e):
        plan_ref[e] = 0

    @pl.loop(0, 64)
    def _(i):
        a, _ = page_of(i, 0)
        b, _ = page_of(i, 1)
        count[a] = count[a] + 1
        count[b] = count[b] + jnp.where(b == a, 0, 1)

    start = jnp.int32(0)
    fill[0] = TRASH
    for r in range(requests):
        fill[r + 1] = 2 * start
        groups = (count[r + 1] + 1) >> 1

        @pl.loop(start, start + groups)
        def _(g):
            plan_ref[8 + g] = r

        start = start + groups
    plan_ref[0] = start

    @pl.loop(0, 64)
    def _(i):
        a, rows_a = page_of(i, 0)
        b, rows_b = page_of(i, 1)
        at = fill[a]
        fill[a] = at + jnp.where(a > 0, 1, 0)
        plan_ref[ENTRIES + at] = i + (rows_a << 8) + (jnp.where(a == b, rows_b, 0) << 16)
        other = jnp.where(a == b, 0, b)
        at = fill[other]
        fill[other] = at + jnp.where(other > 0, 1, 0)
        plan_ref[ENTRIES + at] = i + (rows_b << 16)


def attention_kernel(
    scale, plan_ref, query_ref, own_ref, other_ref, out_ref, staged, query, scores, top, denom, total, cache, sems
):
    copies = [
        pltpu.make_async_copy(own_ref, cache.at[0], sems.at[0]),
        pltpu.make_async_copy(other_ref, cache.at[1], sems.at[1]),
    ]
    for copy in copies:
        copy.start()
    sources, requests, wide = query_ref.shape
    kv = total.shape[2]
    tiles = kv // LANES
    for t in range(wide // LANES):
        columns = query_ref[:, :, t * LANES : (t + 1) * LANES]
        staged[t] = columns.astype(F32).reshape(sources * requests, LANES)
    for r in range(requests):
        at = pl.ds(r, sources, stride=requests)
        for t in range(tiles):
            columns = slice(t * LANES, (t + 1) * LANES)
            query[r, :sources, columns] = staged[t, at, :].astype(BF16)
            query[r, sources:, columns] = staged[tiles + t, at, :].astype(BF16)
        rows = staged[2 * tiles, at, :].astype(BF16)
        query[r, :sources, kv:] = rows[:, :64]
        query[r, sources:, kv:] = rows[:, 64:]
    top[...] = jnp.full_like(top, EMPTY)
    denom[...] = jnp.zeros_like(denom)
    total[...] = jnp.zeros_like(total)
    for copy in copies:
        copy.wait()
    groups = plan_ref[0]
    lane = lax.broadcasted_iota(jnp.int32, (1, 2 * LANES), 1)
    within = lane & (PAGE - 1)

    def keys(g, depth):
        tiles = []
        for side in range(2):
            tile = plan_ref[ENTRIES + 2 * g + side] & 255
            at = pl.multiple_of((tile & 31) * LANES, LANES)
            tiles.append(cache[tile >> 5, :depth, pl.ds(at, LANES)])
        return jnp.concatenate(tiles, axis=1)

    @pl.loop(0, groups)
    def _(g):
        r = plan_ref[8 + g]
        first = plan_ref[ENTRIES + 2 * g]
        second = plan_ref[ENTRIES + 2 * g + 1]
        score = jnp.dot(query[r], keys(g, cache.shape[1]), preferred_element_type=F32)
        rows = jnp.where(
            lane < 2 * PAGE,
            jnp.where(lane < PAGE, (first >> 8) & 255, first >> 16),
            jnp.where(lane < 3 * PAGE, (second >> 8) & 255, second >> 16),
        )
        score = jnp.where(within < rows, score, EMPTY)
        scores[g] = score
        top[r] = jnp.maximum(top[r], jnp.maximum(score[:, :LANES], score[:, LANES:]))

    for r in range(requests):
        top[r] = jnp.broadcast_to(jnp.max(top[r], axis=1, keepdims=True), top.shape[1:])

    @pl.loop(0, groups)
    def _(g):
        r = plan_ref[8 + g]
        level = top[r]
        score = scores[g]
        expo = jnp.concatenate(
            [
                jnp.exp((score[:, :LANES] - level) * scale),
                jnp.exp((score[:, LANES:] - level) * scale),
            ],
            axis=1,
        ).astype(BF16)
        wide_expo = expo.astype(F32)
        denom[r] = denom[r] + wide_expo[:, :LANES] + wide_expo[:, LANES:]
        total[r] = total[r] + lax.dot_general(
            expo, keys(g, kv), (((1,), (1,)), ((), ())), preferred_element_type=F32
        )

    for r in range(requests):
        sums = jnp.sum(denom[r], axis=1, keepdims=True)
        some = sums > 0.0
        safe = jnp.where(some, sums, 1.0)
        level = jnp.where(some, top[r][:, :1] * scale + jnp.log(safe), EMPTY)
        rows = total[r] * (1.0 / safe)
        at = pl.ds(r, sources, stride=requests)
        for t in range(tiles):
            columns = slice(t * LANES, (t + 1) * LANES)
            staged[t, at, :] = rows[:sources, columns]
            staged[tiles + t, at, :] = rows[sources:, columns]
        staged[2 * tiles, at, :] = stat_lanes([level[:sources], level[sources:]], sources)
    for t in range(wide // LANES):
        columns = slice(t * LANES, (t + 1) * LANES)
        out_ref[:, :, columns] = staged[t].reshape(sources, requests, LANES).astype(BF16)


def fold_kernel(core_ref, part_ref, up_ref, out_ref):
    sources, requests, wide = part_ref.shape
    kv = up_ref.shape[1]
    stats = part_ref[:, :, 2 * kv :].astype(F32)
    outputs, levels = [], []
    for j in range(2):
        level = read_stat(stats, j)
        peak = jnp.max(level, axis=0)
        weight = jnp.exp(level - peak[None])
        norm = jnp.sum(weight, axis=0)
        rows = part_ref[:, :, j * kv : (j + 1) * kv].astype(F32)
        rows = jnp.sum(rows * weight, axis=0) / norm
        outputs.append(jnp.dot(rows.astype(BF16), up_ref[j], preferred_element_type=F32))
        levels.append(peak + jnp.log(norm))
    block = jnp.concatenate(outputs + [stat_lanes(levels, requests)], axis=1).astype(BF16)
    for k in range(out_ref.shape[0]):
        out_ref[k] = block


def merge_kernel(part_ref, out_ref):
    width = 2 * LANES
    both = part_ref[...].astype(F32)
    both = both.reshape(both.shape[0] // 2, 2, *both.shape[1:])
    for core in range(2):
        parts = both[:, core]
        stats = parts[:, :, width:]
        for j in range(2):
            level = read_stat(stats, j)
            weight = jnp.exp(level - jnp.max(level, axis=0)[None])
            rows = jnp.sum(parts[:, :, j * LANES : (j + 1) * LANES] * weight, axis=0)
            rows = rows / jnp.sum(weight, axis=0)
            at = (2 * core + j) * LANES
            out_ref[:, at : at + LANES] = rows.astype(BF16)


def vmem():
    return pl.BlockSpec(memory_space=pltpu.VMEM)


def smem():
    return pl.BlockSpec(memory_space=pltpu.SMEM)


def anywhere():
    return pl.BlockSpec(memory_space=pl.ANY)


def params():
    return pltpu.CompilerParams(vmem_limit_bytes=VMEM_LIMIT)


def make_queries(core, nope, rope, key_up, copies):
    heads, requests, width = nope.shape
    kv = key_up.shape[2]
    wide = 2 * kv + 2 * rope.shape[2]
    whole = lambda i, c: (0, 0, 0)
    return pl.pallas_call(
        query_kernel,
        grid_spec=pltpu.PrefetchScalarGridSpec(
            num_scalar_prefetch=1,
            grid=(1,),
            in_specs=[
                pl.BlockSpec(nope.shape, whole),
                pl.BlockSpec(rope.shape, whole),
                pl.BlockSpec((2, width, kv), lambda i, c: (c[0], 0, 0)),
            ],
            out_specs=pl.BlockSpec((copies, requests, wide), whole),
        ),
        out_shape=jax.ShapeDtypeStruct((copies, requests, wide), BF16),
        compiler_params=params(),
        name="queries",
    )(core, nope, rope, key_up)


def make_plan(where, lengths, table):
    return pl.pallas_call(
        plan_kernel,
        out_shape=jax.ShapeDtypeStruct((PLAN,), jnp.int32),
        in_specs=[smem(), smem(), vmem()],
        out_specs=smem(),
        scratch_shapes=[
            pltpu.VMEM((16, LANES), jnp.int32),
            pltpu.SMEM((16, LANES), jnp.int32),
            pltpu.SMEM((16,), jnp.int32),
            pltpu.SMEM((16,), jnp.int32),
            pltpu.SemaphoreType.DMA,
        ],
        compiler_params=params(),
        cost_estimate=pl.CostEstimate(flops=10_000_000, bytes_accessed=4_000_000, transcendentals=0),
        name="plan",
    )(where, lengths, table)


def attend(scale, plan, queries, own, other):
    sources, requests, wide = queries.shape
    width, tokens = own.shape
    kv = (wide - 128) // 2
    heads = 2 * sources
    return pl.pallas_call(
        functools.partial(attention_kernel, scale),
        out_shape=jax.ShapeDtypeStruct((sources, requests, wide), BF16),
        in_specs=[smem(), vmem(), anywhere(), anywhere()],
        out_specs=vmem(),
        scratch_shapes=[
            pltpu.VMEM((wide // LANES, sources * requests, LANES), F32),
            pltpu.VMEM((requests, heads, width), BF16),
            pltpu.VMEM((72, heads, 2 * LANES), F32),
            pltpu.VMEM((requests, heads, LANES), F32),
            pltpu.VMEM((requests, heads, LANES), F32),
            pltpu.VMEM((requests, heads, kv), F32),
            pltpu.VMEM((2, width, tokens), BF16),
            pltpu.SemaphoreType.DMA((2,)),
        ],
        compiler_params=params(),
        cost_estimate=pl.CostEstimate(
            flops=1_200_000_000, bytes_accessed=12_000_000, transcendentals=524_288
        ),
        name="attention",
    )(plan, queries, own, other)


def fold(core, parts, value_up, copies):
    sources, requests, wide = parts.shape
    kv, out = value_up.shape[1:]
    whole = lambda i, c: (0, 0, 0)
    return pl.pallas_call(
        fold_kernel,
        grid_spec=pltpu.PrefetchScalarGridSpec(
            num_scalar_prefetch=1,
            grid=(1,),
            in_specs=[
                pl.BlockSpec(parts.shape, whole),
                pl.BlockSpec((2, kv, out), lambda i, c: (c[0], 0, 0)),
            ],
            out_specs=pl.BlockSpec((copies, requests, 3 * LANES), whole),
        ),
        out_shape=jax.ShapeDtypeStruct((copies, requests, 3 * LANES), BF16),
        compiler_params=params(),
        name="fold",
    )(core, parts, value_up)


def merge(parts):
    requests = parts.shape[1]
    return pl.pallas_call(
        merge_kernel,
        out_shape=jax.ShapeDtypeStruct((requests, 4 * LANES), BF16),
        in_specs=[vmem()],
        out_specs=vmem(),
        compiler_params=params(),
        name="merge",
    )(parts)


def local(query_nope, query_rope, key_up, value_up, cache, lengths, table):
    scale = float(query_nope.shape[2] + query_rope.shape[2]) ** -0.5
    rows, cols = lax.axis_size("row"), lax.axis_size("col")
    column = lax.axis_index("col")
    core = (column % 2).astype(jnp.int32)
    chip = lax.axis_index("row") * (cols // 2) + column // 2
    own = cache.T
    swap = [(i, i ^ 1) for i in range(cols)]
    other = lax.ppermute(own, "col", swap)
    queries = make_queries(
        core[None], jnp.swapaxes(query_nope, 0, 1), jnp.swapaxes(query_rope, 0, 1), key_up, rows
    )
    queries = lax.all_to_all(queries, "row", split_axis=0, concat_axis=0, tiled=True)
    where = jnp.stack([chip * 128, core]).astype(jnp.int32)
    plan = make_plan(where, lengths, table)
    parts = attend(scale, plan, queries, own, other)
    parts = lax.all_to_all(parts, "row", split_axis=0, concat_axis=0, tiled=True)
    parts = fold(core[None], parts, value_up, cols)
    parts = lax.all_to_all(parts, "col", split_axis=0, concat_axis=0, tiled=True)
    return merge(parts)


def solution(mesh):
    placed = (
        P(None, "row", None),
        P(None, "row", None),
        P("row", None, None),
        P("row", None, None),
        P(("row", "col"), None),
        P(),
        P(),
    )
    return jax.shard_map(
        local, mesh=mesh, in_specs=placed, out_specs=P(None, "row"), check_vma=False
    )
```

```python
import functools

import jax
import jax.numpy as jnp
from jax import lax
from jax.experimental import pallas as pl
from jax.experimental.pallas import tpu as pltpu
from jax.sharding import PartitionSpec as P

PAGE = 64
LANES = 128
EMPTY = -1e30
UNROLL = 4
GROUPS = 40
STEPS = GROUPS // UNROLL
CHUNK = UNROLL * 2 * LANES
MIB = 1024 * 1024
ALL_VMEM = 40 * MIB
ENTRIES = 64
TRASH = 180
PLAN = 256
F32 = jnp.float32
BF16 = jnp.bfloat16


def three_terms(value):
    high = value.astype(BF16)
    rest = value - high.astype(F32)
    middle = rest.astype(BF16)
    low = (rest - middle.astype(F32)).astype(BF16)
    return high, middle, low


def stat_lanes(values, rows):
    lane = lax.broadcasted_iota(jnp.int32, (rows, LANES), 1)
    out = jnp.zeros((rows, LANES), F32)
    for head, value in enumerate(values):
        for at, term in enumerate(three_terms(value)):
            out = jnp.where(lane == 64 * head + at, term.astype(F32), out)
    return out


def read_stat(lanes, head):
    at = 64 * head
    return lanes[..., at : at + 1] + lanes[..., at + 1 : at + 2] + lanes[..., at + 2 : at + 3]


def query_kernel(nope_any, rope_any, up_ref, out_ref, nope_ref, rope_ref, up, row, sems, out_sems):
    copies, requests, _ = out_ref.shape
    first = 2 * (lax.axis_index("col") & 1)
    loads = [
        pltpu.make_async_copy(nope_any, nope_ref, sems.at[0]),
        pltpu.make_async_copy(rope_any, rope_ref, sems.at[1]),
        pltpu.make_async_copy(up_ref.at[pl.ds(first, 2)], up, sems.at[2]),
    ]
    for load in loads:
        load.start()

    def head_of(ref, j):
        rows = ref[...].astype(F32)
        head = lax.broadcasted_iota(jnp.int32, rows.shape, 1)
        return jnp.sum(jnp.where(head == first + j, rows, 0.0), axis=1).astype(BF16)

    loads[0].wait()
    nopes = [head_of(nope_ref, j) for j in range(2)]
    loads[1].wait()
    ropes = [head_of(rope_ref, j) for j in range(2)]
    loads[2].wait()
    parts = [
        jnp.dot(nopes[j], up[j], preferred_element_type=F32).astype(BF16) for j in range(2)
    ]
    row[...] = jnp.concatenate(parts + ropes, axis=1)
    stores = [
        pltpu.make_async_copy(row, out_ref.at[k], out_sems.at[k]) for k in range(copies)
    ]
    for store in stores:
        store.start()
    for store in stores:
        store.wait()


def gather_kernel(
    length_ref,
    table_any,
    own_ref,
    other_ref,
    plan_ref,
    keys_ref,
    table_ref,
    cache,
    keys,
    vec,
    sm,
    count,
    fill,
    sem,
    cache_sems,
    out_sems,
):
    loads = [
        pltpu.make_async_copy(own_ref, cache.at[0], cache_sems.at[0]),
        pltpu.make_async_copy(other_ref, cache.at[1], cache_sems.at[1]),
    ]
    copy = pltpu.make_async_copy(table_any, table_ref, sem)
    copy.start()
    for load in loads:
        load.start()
    copy.wait()
    column = lax.axis_index("col")
    core = column & 1
    chip = lax.axis_index("row") * (lax.axis_size("col") // 2) + (column >> 1)
    base = chip * 128
    requests, width = table_ref.shape
    page = lax.broadcasted_iota(jnp.int32, (1, width), 1)
    high = lax.broadcasted_iota(jnp.int32, (8, width), 0)
    low = lax.broadcasted_iota(jnp.int32, (16, width), 0)
    total = jnp.zeros((16, 16), F32)
    for r in range(requests):
        slot = table_ref[r : r + 1, :] - base
        live = jnp.clip(length_ref[r] - page * PAGE, 0, PAGE).astype(F32)
        hit = high == (slot >> 4)
        owner = jnp.where(hit, float(r + 1), 0.0)
        rows = jnp.where(hit, live, 0.0)
        left = jnp.concatenate([owner, rows], axis=0).astype(BF16)
        right = jnp.where(low == (slot & 15), 1.0, 0.0).astype(BF16)
        total = total + lax.dot_general(
            left, right, (((1,), (1,)), ((), ())), preferred_element_type=F32
        )
    vec[:, :16] = total.astype(jnp.int32)
    copy = pltpu.make_async_copy(vec, sm, sem)
    copy.start()
    copy.wait()

    def page_of(i, side):
        s = (2 * i + side + PAGE * core) & 127
        return sm[s >> 4, s & 15], sm[8 + (s >> 4), s & 15]

    for r in range(16):
        count[r] = 0

    def page_of(t):
        s = (t + PAGE * core) & 127
        return sm[s >> 4, s & 15], sm[8 + (s >> 4), s & 15]

    @pl.loop(0, 128, unroll=16)
    def _(t):
        owner, _ = page_of(t)
        count[owner] = count[owner] + 1

    start = jnp.int32(0)
    fill[0] = TRASH
    for r in range(requests):
        fill[r + 1] = 4 * start
        groups = (count[r + 1] + 3) >> 2

        @pl.loop(start, start + groups)
        def _(g):
            plan_ref[8 + g] = r
            for at in range(4):
                plan_ref[ENTRIES + 4 * g + at] = 0

        start = start + groups
    plan_ref[0] = start
    for ahead in range(UNROLL - 1):
        plan_ref[8 + start + ahead] = 0
        for at in range(4):
            plan_ref[ENTRIES + 4 * (start + ahead) + at] = 0

    @pl.loop(0, 128, unroll=8)
    def _(t):
        owner, rows = page_of(t)
        at = fill[owner]
        fill[owner] = at + jnp.where(owner > 0, 1, 0)
        plan_ref[ENTRIES + at] = t + (rows << 8)

    for load in loads:
        load.wait()
    steps = (plan_ref[0] + UNROLL - 1) // UNROLL
    left_half = lax.broadcasted_iota(jnp.int32, (1, LANES), 1) < PAGE

    def tile_of(entry):
        slot = entry & 127
        at = pl.multiple_of(((slot & 63) >> 1) * LANES, LANES)
        return cache[slot >> 6, :, pl.ds(at, LANES)]

    def turned(tile):
        return jnp.concatenate([tile[:, PAGE:], tile[:, :PAGE]], axis=1)

    def chunk(step):
        at = pl.ds(pl.multiple_of(step * CHUNK, CHUNK), CHUNK)
        return pltpu.make_async_copy(keys.at[:, at], keys_ref.at[:, at], out_sems.at[step])

    @pl.loop(0, steps)
    def _(step):
        @pl.loop(step * 2 * UNROLL, (step + 1) * 2 * UNROLL)
        def _(j):
            first = plan_ref[ENTRIES + 2 * j]
            second = plan_ref[ENTRIES + 2 * j + 1]
            kind = (first & 1) + 2 * (second & 1)
            at = pl.ds(pl.multiple_of(j * LANES, LANES), LANES)

            @pl.when(kind == 2)
            def _():
                keys[:, at] = jnp.where(left_half, tile_of(first), tile_of(second))

            @pl.when(kind == 0)
            def _():
                keys[:, at] = jnp.where(left_half, tile_of(first), turned(tile_of(second)))

            @pl.when(kind == 3)
            def _():
                keys[:, at] = jnp.where(left_half, turned(tile_of(first)), tile_of(second))

            @pl.when(kind == 1)
            def _():
                keys[:, at] = turned(jnp.where(left_half, tile_of(second), tile_of(first)))

        chunk(step).start()

    @pl.loop(0, steps)
    def _(step):
        chunk(step).wait()


def attention_kernel(
    scale, plan_ref, query_any, keys_any, out_ref, query_ref, query_sem, staged, query, scores, top, denom, total, keys_ref, sems
):
    load = pltpu.make_async_copy(query_any, query_ref, query_sem)
    load.start()
    groups = plan_ref[0]
    steps = (groups + UNROLL - 1) // UNROLL

    def chunk(step):
        at = pl.ds(pl.multiple_of(step * CHUNK, CHUNK), CHUNK)
        return pltpu.make_async_copy(keys_any.at[:, at], keys_ref.at[:, at], sems.at[step])

    @pl.loop(0, steps)
    def _(step):
        chunk(step).start()

    sources, requests, wide = query_ref.shape
    kv = total.shape[2]
    tiles = kv // LANES
    top[...] = jnp.full_like(top, EMPTY)
    denom[...] = jnp.zeros_like(denom)
    total[...] = jnp.zeros_like(total)
    load.wait()
    for t in range(wide // LANES):
        columns = query_ref[:, :, t * LANES : (t + 1) * LANES]
        staged[t] = columns.astype(F32).reshape(sources * requests, LANES)
    for r in range(requests):
        at = pl.ds(r, sources, stride=requests)
        for t in range(tiles):
            columns = slice(t * LANES, (t + 1) * LANES)
            query[r, :sources, columns] = staged[t, at, :].astype(BF16)
            query[r, sources:, columns] = staged[tiles + t, at, :].astype(BF16)
        rows = staged[2 * tiles, at, :].astype(BF16)
        query[r, :sources, kv:] = rows[:, :64]
        query[r, sources:, kv:] = rows[:, 64:]
    lane = lax.broadcasted_iota(jnp.int32, (1, LANES), 1)
    left_half = lane < PAGE
    within = lane & (PAGE - 1)

    def keys(g, depth):
        return keys_ref[:depth, pl.ds(pl.multiple_of(g * 2 * LANES, 2 * LANES), 2 * LANES)]

    @pl.loop(0, steps)
    def _(step):
        chunk(step).wait()
        for u in range(UNROLL):
            g = step * UNROLL + u
            r = plan_ref[8 + g]
            score = jnp.dot(query[r], keys(g, keys_ref.shape[0]), preferred_element_type=F32)
            halves = []
            for half in range(2):
                rows = jnp.where(
                    left_half,
                    plan_ref[ENTRIES + 4 * g + 2 * half] >> 8,
                    plan_ref[ENTRIES + 4 * g + 2 * half + 1] >> 8,
                )
                part = score[:, half * LANES : (half + 1) * LANES]
                part = jnp.where(within < rows, part, EMPTY)
                scores[g, :, half * LANES : (half + 1) * LANES] = part
                halves.append(part)
            top[r] = jnp.maximum(top[r], jnp.maximum(*halves))

    for r in range(requests):
        top[r] = jnp.broadcast_to(jnp.max(top[r], axis=1, keepdims=True), top.shape[1:])

    @pl.loop(0, steps)
    def _(step):
        for u in range(UNROLL):
            g = step * UNROLL + u
            r = plan_ref[8 + g]
            level = top[r]
            live = jnp.where(g < groups, 1.0, 0.0)
            halves = []
            for half in range(2):
                part = scores[g, :, half * LANES : (half + 1) * LANES]
                halves.append((jnp.exp((part - level) * scale) * live).astype(BF16))
            denom[r] = denom[r] + halves[0].astype(F32) + halves[1].astype(F32)
            total[r] = total[r] + lax.dot_general(
                jnp.concatenate(halves, axis=1),
                keys(g, kv),
                (((1,), (1,)), ((), ())),
                preferred_element_type=F32,
            )

    for r in range(requests):
        sums = jnp.sum(denom[r], axis=1, keepdims=True)
        some = sums > 0.0
        safe = jnp.where(some, sums, 1.0)
        level = jnp.where(some, top[r][:, :1] * scale + jnp.log(safe), EMPTY)
        rows = total[r] * (1.0 / safe)
        at = pl.ds(r, sources, stride=requests)
        for t in range(tiles):
            columns = slice(t * LANES, (t + 1) * LANES)
            staged[t, at, :] = rows[:sources, columns]
            staged[tiles + t, at, :] = rows[sources:, columns]
        staged[2 * tiles, at, :] = stat_lanes([level[:sources], level[sources:]], sources)
    for t in range(wide // LANES):
        columns = slice(t * LANES, (t + 1) * LANES)
        out_ref[:, :, columns] = staged[t].reshape(sources, requests, LANES).astype(BF16)


def fold_kernel(part_ref, up_any, out_ref, up_ref, sem):
    first = 2 * (lax.axis_index("col") & 1)
    load = pltpu.make_async_copy(up_any.at[pl.ds(first, 2)], up_ref, sem)
    load.start()
    sources, requests, wide = part_ref.shape
    kv = up_ref.shape[1]
    stats = part_ref[:, :, 2 * kv :].astype(F32)
    outputs, levels = [], []
    for j in range(2):
        level = read_stat(stats, j)
        peak = jnp.max(level, axis=0)
        weight = jnp.exp(level - peak[None])
        norm = jnp.sum(weight, axis=0)
        rows = part_ref[:, :, j * kv : (j + 1) * kv].astype(F32)
        rows = jnp.sum(rows * weight, axis=0) / norm
        if j == 0:
            load.wait()
        outputs.append(jnp.dot(rows.astype(BF16), up_ref[j], preferred_element_type=F32))
        levels.append(peak + jnp.log(norm))
    block = jnp.concatenate(outputs + [stat_lanes(levels, requests)], axis=1).astype(BF16)
    for k in range(out_ref.shape[0]):
        out_ref[k] = block


def merge_kernel(part_ref, out_ref):
    width = 2 * LANES
    both = part_ref[...].astype(F32)
    both = both.reshape(both.shape[0] // 2, 2, *both.shape[1:])
    for core in range(2):
        parts = both[:, core]
        stats = parts[:, :, width:]
        for j in range(2):
            level = read_stat(stats, j)
            weight = jnp.exp(level - jnp.max(level, axis=0)[None])
            rows = jnp.sum(parts[:, :, j * LANES : (j + 1) * LANES] * weight, axis=0)
            rows = rows / jnp.sum(weight, axis=0)
            at = (2 * core + j) * LANES
            out_ref[:, at : at + LANES] = rows.astype(BF16)


def vmem():
    return pl.BlockSpec(memory_space=pltpu.VMEM)


def smem():
    return pl.BlockSpec(memory_space=pltpu.SMEM)


def anywhere():
    return pl.BlockSpec(memory_space=pl.ANY)


def params(limit=32 * MIB):
    return pltpu.CompilerParams(vmem_limit_bytes=limit)


def make_queries(nope, rope, key_up, copies):
    requests, heads, width = nope.shape
    kv = key_up.shape[2]
    wide = 2 * kv + 2 * rope.shape[2]
    return pl.pallas_call(
        query_kernel,
        out_shape=jax.ShapeDtypeStruct((copies, requests, wide), BF16),
        in_specs=[anywhere(), anywhere(), anywhere()],
        out_specs=anywhere(),
        scratch_shapes=[
            pltpu.VMEM(nope.shape, BF16),
            pltpu.VMEM(rope.shape, BF16),
            pltpu.VMEM((2, width, kv), BF16),
            pltpu.VMEM((requests, wide), BF16),
            pltpu.SemaphoreType.DMA((3,)),
            pltpu.SemaphoreType.DMA((copies,)),
        ],
        compiler_params=params(ALL_VMEM),
        name="queries",
    )(nope, rope, key_up)


def gather(lengths, table, own, other):
    width, tokens = own.shape
    return pl.pallas_call(
        gather_kernel,
        out_shape=(
            jax.ShapeDtypeStruct((PLAN,), jnp.int32),
            jax.ShapeDtypeStruct((width, STEPS * CHUNK), BF16),
        ),
        in_specs=[smem(), anywhere(), anywhere(), anywhere()],
        out_specs=(smem(), anywhere()),
        scratch_shapes=[
            pltpu.VMEM(table.shape, jnp.int32),
            pltpu.VMEM((2, width, tokens), BF16),
            pltpu.VMEM((width, STEPS * CHUNK), BF16),
            pltpu.VMEM((16, LANES), jnp.int32),
            pltpu.SMEM((16, LANES), jnp.int32),
            pltpu.SMEM((16,), jnp.int32),
            pltpu.SMEM((16,), jnp.int32),
            pltpu.SemaphoreType.DMA,
            pltpu.SemaphoreType.DMA((2,)),
            pltpu.SemaphoreType.DMA((STEPS,)),
        ],
        compiler_params=params(ALL_VMEM),
        cost_estimate=pl.CostEstimate(
            flops=10_000_000, bytes_accessed=20_000_000, transcendentals=0
        ),
        name="gather",
    )(lengths, table, own, other)


def attend(scale, plan, queries, keys):
    sources, requests, wide = queries.shape
    width = keys.shape[0]
    kv = (wide - 128) // 2
    heads = 2 * sources
    return pl.pallas_call(
        functools.partial(attention_kernel, scale),
        out_shape=jax.ShapeDtypeStruct((sources, requests, wide), BF16),
        in_specs=[smem(), anywhere(), anywhere()],
        out_specs=vmem(),
        scratch_shapes=[
            pltpu.VMEM(queries.shape, BF16),
            pltpu.SemaphoreType.DMA,
            pltpu.VMEM((wide // LANES, sources * requests, LANES), F32),
            pltpu.VMEM((requests, heads, width), BF16),
            pltpu.VMEM((GROUPS, heads, 2 * LANES), F32),
            pltpu.VMEM((requests, heads, LANES), F32),
            pltpu.VMEM((requests, heads, LANES), F32),
            pltpu.VMEM((requests, heads, kv), F32),
            pltpu.VMEM(keys.shape, BF16),
            pltpu.SemaphoreType.DMA((STEPS,)),
        ],
        compiler_params=params(40 * MIB),
        cost_estimate=pl.CostEstimate(
            flops=1_200_000_000, bytes_accessed=12_000_000, transcendentals=524_288
        ),
        name="attention",
    )(plan, queries, keys)


def fold(parts, value_up, copies):
    sources, requests, wide = parts.shape
    kv, out = value_up.shape[1:]
    return pl.pallas_call(
        fold_kernel,
        out_shape=jax.ShapeDtypeStruct((copies, requests, 3 * LANES), BF16),
        in_specs=[vmem(), anywhere()],
        out_specs=vmem(),
        scratch_shapes=[pltpu.VMEM((2, kv, out), BF16), pltpu.SemaphoreType.DMA],
        compiler_params=params(),
        name="fold",
    )(parts, value_up)


def merge(parts):
    requests = parts.shape[1]
    return pl.pallas_call(
        merge_kernel,
        out_shape=jax.ShapeDtypeStruct((requests, 4 * LANES), BF16),
        in_specs=[vmem()],
        out_specs=vmem(),
        compiler_params=params(),
        name="merge",
    )(parts)


def local(query_nope, query_rope, key_up, value_up, cache, lengths, table):
    scale = float(query_nope.shape[2] + query_rope.shape[2]) ** -0.5
    rows, cols = lax.axis_size("row"), lax.axis_size("col")
    own = cache.T
    other = lax.ppermute(own, "col", [(i, i ^ 1) for i in range(cols)])
    queries = make_queries(query_nope, query_rope, key_up, rows)
    queries = lax.all_to_all(queries, "row", split_axis=0, concat_axis=0, tiled=True)
    plan, keys = gather(lengths, table, own, other)
    parts = attend(scale, plan, queries, keys)
    parts = lax.all_to_all(parts, "row", split_axis=0, concat_axis=0, tiled=True)
    parts = fold(parts, value_up, cols)
    parts = lax.all_to_all(parts, "col", split_axis=0, concat_axis=0, tiled=True)
    return merge(parts)


def solution(mesh):
    placed = (
        P(None, "row", None),
        P(None, "row", None),
        P("row", None, None),
        P("row", None, None),
        P(("row", "col"), None),
        P(),
        P(),
    )
    return jax.shard_map(
        local, mesh=mesh, in_specs=placed, out_specs=P(None, "row"), check_vma=False
    )
```

```python
import functools

import jax
import jax.numpy as jnp
from jax import lax
from jax.experimental import pallas as pl
from jax.experimental.pallas import tpu as pltpu
from jax.sharding import PartitionSpec as P

PAGE = 64
LANES = 128
EMPTY = -1e30
UNROLL = 4
GROUPS = 40
STEPS = GROUPS // UNROLL
CHUNK = UNROLL * 2 * LANES
MIB = 1024 * 1024
ALL_VMEM = 60 * MIB
ENTRIES = 64
TRASH = 180
PLAN = 256
F32 = jnp.float32
BF16 = jnp.bfloat16


def three_terms(value):
    high = value.astype(BF16)
    rest = value - high.astype(F32)
    middle = rest.astype(BF16)
    low = (rest - middle.astype(F32)).astype(BF16)
    return high, middle, low


def stat_lanes(values, rows):
    lane = lax.broadcasted_iota(jnp.int32, (rows, LANES), 1)
    out = jnp.zeros((rows, LANES), F32)
    for head, value in enumerate(values):
        for at, term in enumerate(three_terms(value)):
            out = jnp.where(lane == 64 * head + at, term.astype(F32), out)
    return out


def read_stat(lanes, head):
    at = 64 * head
    return lanes[..., at : at + 1] + lanes[..., at + 1 : at + 2] + lanes[..., at + 2 : at + 3]


def query_kernel(nope_any, rope_any, up_ref, out_ref, nope_ref, rope_ref, up, row, sems, out_sems):
    copies, requests, _ = out_ref.shape
    first = 2 * (lax.axis_index("col") & 1)
    loads = [
        pltpu.make_async_copy(nope_any, nope_ref, sems.at[0]),
        pltpu.make_async_copy(rope_any, rope_ref, sems.at[1]),
        pltpu.make_async_copy(up_ref.at[pl.ds(first, 2)], up, sems.at[2]),
    ]
    for load in loads:
        load.start()

    def head_of(ref, j):
        rows = ref[...].astype(F32)
        head = lax.broadcasted_iota(jnp.int32, rows.shape, 1)
        return jnp.sum(jnp.where(head == first + j, rows, 0.0), axis=1).astype(BF16)

    loads[0].wait()
    nopes = [head_of(nope_ref, j) for j in range(2)]
    loads[1].wait()
    ropes = [head_of(rope_ref, j) for j in range(2)]
    loads[2].wait()
    parts = [
        jnp.dot(nopes[j], up[j], preferred_element_type=F32).astype(BF16) for j in range(2)
    ]
    row[...] = jnp.concatenate(parts + ropes, axis=1)
    stores = [
        pltpu.make_async_copy(row, out_ref.at[k], out_sems.at[k]) for k in range(copies)
    ]
    for store in stores:
        store.start()
    for store in stores:
        store.wait()


def gather_kernel(
    length_ref,
    table_any,
    own_ref,
    other_ref,
    plan_ref,
    keys_ref,
    table_ref,
    cache,
    keys,
    vec,
    sm,
    count,
    fill,
    sem,
    cache_sems,
    out_sems,
):
    loads = [
        pltpu.make_async_copy(own_ref, cache.at[0], cache_sems.at[0]),
        pltpu.make_async_copy(other_ref, cache.at[1], cache_sems.at[1]),
    ]
    copy = pltpu.make_async_copy(table_any, table_ref, sem)
    copy.start()
    for load in loads:
        load.start()
    copy.wait()
    column = lax.axis_index("col")
    core = column & 1
    chip = lax.axis_index("row") * (lax.axis_size("col") // 2) + (column >> 1)
    base = chip * 128
    requests, width = table_ref.shape
    page = lax.broadcasted_iota(jnp.int32, (1, width), 1)
    high = lax.broadcasted_iota(jnp.int32, (8, width), 0)
    low = lax.broadcasted_iota(jnp.int32, (16, width), 0)
    total = jnp.zeros((16, 16), F32)
    for r in range(requests):
        slot = table_ref[r : r + 1, :] - base
        live = jnp.clip(length_ref[r] - page * PAGE, 0, PAGE).astype(F32)
        hit = high == (slot >> 4)
        owner = jnp.where(hit, float(r + 1), 0.0)
        rows = jnp.where(hit, live, 0.0)
        left = jnp.concatenate([owner, rows], axis=0).astype(BF16)
        right = jnp.where(low == (slot & 15), 1.0, 0.0).astype(BF16)
        total = total + lax.dot_general(
            left, right, (((1,), (1,)), ((), ())), preferred_element_type=F32
        )
    vec[:, :16] = total.astype(jnp.int32)
    copy = pltpu.make_async_copy(vec, sm, sem)
    copy.start()
    copy.wait()

    def page_of(i, side):
        s = (2 * i + side + PAGE * core) & 127
        return sm[s >> 4, s & 15], sm[8 + (s >> 4), s & 15]

    for r in range(16):
        count[r] = 0

    def page_of(t):
        s = (t + PAGE * core) & 127
        return sm[s >> 4, s & 15], sm[8 + (s >> 4), s & 15]

    @pl.loop(0, 128, unroll=16)
    def _(t):
        owner, _ = page_of(t)
        count[owner] = count[owner] + 1

    start = jnp.int32(0)
    fill[0] = TRASH
    for r in range(requests):
        fill[r + 1] = 4 * start
        groups = (count[r + 1] + 3) >> 2

        @pl.loop(start, start + groups)
        def _(g):
            plan_ref[8 + g] = r
            for at in range(4):
                plan_ref[ENTRIES + 4 * g + at] = 0

        start = start + groups
    plan_ref[0] = start
    for ahead in range(UNROLL - 1):
        plan_ref[8 + start + ahead] = 0
        for at in range(4):
            plan_ref[ENTRIES + 4 * (start + ahead) + at] = 0

    @pl.loop(0, 128, unroll=8)
    def _(t):
        owner, rows = page_of(t)
        at = fill[owner]
        fill[owner] = at + jnp.where(owner > 0, 1, 0)
        plan_ref[ENTRIES + at] = t + (rows << 8)

    for load in loads:
        load.wait()
    steps = (plan_ref[0] + UNROLL - 1) // UNROLL
    left_half = lax.broadcasted_iota(jnp.int32, (1, LANES), 1) < PAGE

    def tile_of(entry):
        slot = entry & 127
        at = pl.multiple_of(((slot & 63) >> 1) * LANES, LANES)
        return cache[slot >> 6, :, pl.ds(at, LANES)]

    def turned(tile):
        return jnp.concatenate([tile[:, PAGE:], tile[:, :PAGE]], axis=1)

    def chunk(step):
        at = pl.ds(pl.multiple_of(step * CHUNK, CHUNK), CHUNK)
        return pltpu.make_async_copy(keys.at[:, at], keys_ref.at[:, at], out_sems.at[step])

    @pl.loop(0, steps)
    def _(step):
        @pl.loop(step * 2 * UNROLL, (step + 1) * 2 * UNROLL)
        def _(j):
            first = plan_ref[ENTRIES + 2 * j]
            second = plan_ref[ENTRIES + 2 * j + 1]
            kind = (first & 1) + 2 * (second & 1)
            at = pl.ds(pl.multiple_of(j * LANES, LANES), LANES)

            @pl.when(kind == 2)
            def _():
                keys[:, at] = jnp.where(left_half, tile_of(first), tile_of(second))

            @pl.when(kind == 0)
            def _():
                keys[:, at] = jnp.where(left_half, tile_of(first), turned(tile_of(second)))

            @pl.when(kind == 3)
            def _():
                keys[:, at] = jnp.where(left_half, turned(tile_of(first)), tile_of(second))

            @pl.when(kind == 1)
            def _():
                keys[:, at] = turned(jnp.where(left_half, tile_of(second), tile_of(first)))

        chunk(step).start()

    @pl.loop(0, steps)
    def _(step):
        chunk(step).wait()


def attention_kernel(
    scale, plan_ref, query_any, keys_any, out_ref, query_ref, query_sem, staged, query, scores, top, denom, total, keys_ref, sems
):
    load = pltpu.make_async_copy(query_any, query_ref, query_sem)
    load.start()
    groups = plan_ref[0]
    steps = (groups + UNROLL - 1) // UNROLL

    def chunk(step):
        at = pl.ds(pl.multiple_of(step * CHUNK, CHUNK), CHUNK)
        return pltpu.make_async_copy(keys_any.at[:, at], keys_ref.at[:, at], sems.at[step])

    @pl.loop(0, steps)
    def _(step):
        chunk(step).start()

    sources, requests, wide = query_ref.shape
    kv = total.shape[2]
    tiles = kv // LANES
    top[...] = jnp.full_like(top, EMPTY)
    denom[...] = jnp.zeros_like(denom)
    total[...] = jnp.zeros_like(total)
    load.wait()
    for t in range(wide // LANES):
        columns = query_ref[:, :, t * LANES : (t + 1) * LANES]
        staged[t] = columns.astype(F32).reshape(sources * requests, LANES)
    for r in range(requests):
        at = pl.ds(r, sources, stride=requests)
        for t in range(tiles):
            columns = slice(t * LANES, (t + 1) * LANES)
            query[r, :sources, columns] = staged[t, at, :].astype(BF16)
            query[r, sources:, columns] = staged[tiles + t, at, :].astype(BF16)
        rows = staged[2 * tiles, at, :].astype(BF16)
        query[r, :sources, kv:] = rows[:, :64]
        query[r, sources:, kv:] = rows[:, 64:]
    lane = lax.broadcasted_iota(jnp.int32, (1, LANES), 1)
    left_half = lane < PAGE
    within = lane & (PAGE - 1)

    def keys(g, depth):
        return keys_ref[:depth, pl.ds(pl.multiple_of(g * 2 * LANES, 2 * LANES), 2 * LANES)]

    @pl.loop(0, steps)
    def _(step):
        chunk(step).wait()
        for u in range(UNROLL):
            g = step * UNROLL + u
            r = plan_ref[8 + g]
            score = jnp.dot(query[r], keys(g, keys_ref.shape[0]), preferred_element_type=F32)
            halves = []
            for half in range(2):
                rows = jnp.where(
                    left_half,
                    plan_ref[ENTRIES + 4 * g + 2 * half] >> 8,
                    plan_ref[ENTRIES + 4 * g + 2 * half + 1] >> 8,
                )
                part = score[:, half * LANES : (half + 1) * LANES]
                part = jnp.where(within < rows, part, EMPTY)
                scores[g, :, half * LANES : (half + 1) * LANES] = part
                halves.append(part)
            top[r] = jnp.maximum(top[r], jnp.maximum(*halves))

    for r in range(requests):
        top[r] = jnp.broadcast_to(jnp.max(top[r], axis=1, keepdims=True), top.shape[1:])

    @pl.loop(0, steps)
    def _(step):
        for u in range(UNROLL):
            g = step * UNROLL + u
            r = plan_ref[8 + g]
            level = top[r]
            live = jnp.where(g < groups, 1.0, 0.0)
            halves = []
            for half in range(2):
                part = scores[g, :, half * LANES : (half + 1) * LANES]
                halves.append((jnp.exp((part - level) * scale) * live).astype(BF16))
            denom[r] = denom[r] + halves[0].astype(F32) + halves[1].astype(F32)
            total[r] = total[r] + lax.dot_general(
                jnp.concatenate(halves, axis=1),
                keys(g, kv),
                (((1,), (1,)), ((), ())),
                preferred_element_type=F32,
            )

    for r in range(requests):
        sums = jnp.sum(denom[r], axis=1, keepdims=True)
        some = sums > 0.0
        safe = jnp.where(some, sums, 1.0)
        level = jnp.where(some, top[r][:, :1] * scale + jnp.log(safe), EMPTY)
        rows = total[r] * (1.0 / safe)
        at = pl.ds(r, sources, stride=requests)
        for t in range(tiles):
            columns = slice(t * LANES, (t + 1) * LANES)
            staged[t, at, :] = rows[:sources, columns]
            staged[tiles + t, at, :] = rows[sources:, columns]
        staged[2 * tiles, at, :] = stat_lanes([level[:sources], level[sources:]], sources)
    for t in range(wide // LANES):
        columns = slice(t * LANES, (t + 1) * LANES)
        out_ref[:, :, columns] = staged[t].reshape(sources, requests, LANES).astype(BF16)


def fold_kernel(part_ref, up_any, out_ref, up_ref, sem):
    first = 2 * (lax.axis_index("col") & 1)
    load = pltpu.make_async_copy(up_any.at[pl.ds(first, 2)], up_ref, sem)
    load.start()
    sources, requests, wide = part_ref.shape
    kv = up_ref.shape[1]
    stats = part_ref[:, :, 2 * kv :].astype(F32)
    outputs, levels = [], []
    for j in range(2):
        level = read_stat(stats, j)
        peak = jnp.max(level, axis=0)
        weight = jnp.exp(level - peak[None])
        norm = jnp.sum(weight, axis=0)
        rows = part_ref[:, :, j * kv : (j + 1) * kv].astype(F32)
        rows = jnp.sum(rows * weight, axis=0) / norm
        if j == 0:
            load.wait()
        outputs.append(jnp.dot(rows.astype(BF16), up_ref[j], preferred_element_type=F32))
        levels.append(peak + jnp.log(norm))
    block = jnp.concatenate(outputs + [stat_lanes(levels, requests)], axis=1).astype(BF16)
    for k in range(out_ref.shape[0]):
        out_ref[k] = block


def merge_kernel(part_ref, out_ref):
    width = 2 * LANES
    both = part_ref[...].astype(F32)
    both = both.reshape(both.shape[0] // 2, 2, *both.shape[1:])
    for core in range(2):
        parts = both[:, core]
        stats = parts[:, :, width:]
        for j in range(2):
            level = read_stat(stats, j)
            weight = jnp.exp(level - jnp.max(level, axis=0)[None])
            rows = jnp.sum(parts[:, :, j * LANES : (j + 1) * LANES] * weight, axis=0)
            rows = rows / jnp.sum(weight, axis=0)
            at = (2 * core + j) * LANES
            out_ref[:, at : at + LANES] = rows.astype(BF16)


def vmem():
    return pl.BlockSpec(memory_space=pltpu.VMEM)


def smem():
    return pl.BlockSpec(memory_space=pltpu.SMEM)


def anywhere():
    return pl.BlockSpec(memory_space=pl.ANY)


def params(limit=32 * MIB):
    return pltpu.CompilerParams(vmem_limit_bytes=limit)


def make_queries(nope, rope, key_up, copies):
    requests, heads, width = nope.shape
    kv = key_up.shape[2]
    wide = 2 * kv + 2 * rope.shape[2]
    return pl.pallas_call(
        query_kernel,
        out_shape=jax.ShapeDtypeStruct((copies, requests, wide), BF16),
        in_specs=[anywhere(), anywhere(), anywhere()],
        out_specs=anywhere(),
        scratch_shapes=[
            pltpu.VMEM(nope.shape, BF16),
            pltpu.VMEM(rope.shape, BF16),
            pltpu.VMEM((2, width, kv), BF16),
            pltpu.VMEM((requests, wide), BF16),
            pltpu.SemaphoreType.DMA((3,)),
            pltpu.SemaphoreType.DMA((copies,)),
        ],
        compiler_params=params(ALL_VMEM),
        name="queries",
    )(nope, rope, key_up)


def gather(lengths, table, own, other):
    width, tokens = own.shape
    return pl.pallas_call(
        gather_kernel,
        out_shape=(
            jax.ShapeDtypeStruct((PLAN,), jnp.int32),
            jax.ShapeDtypeStruct((width, STEPS * CHUNK), BF16),
        ),
        in_specs=[smem(), anywhere(), anywhere(), anywhere()],
        out_specs=(smem(), anywhere()),
        scratch_shapes=[
            pltpu.VMEM(table.shape, jnp.int32),
            pltpu.VMEM((2, width, tokens), BF16),
            pltpu.VMEM((width, STEPS * CHUNK), BF16),
            pltpu.VMEM((16, LANES), jnp.int32),
            pltpu.SMEM((16, LANES), jnp.int32),
            pltpu.SMEM((16,), jnp.int32),
            pltpu.SMEM((16,), jnp.int32),
            pltpu.SemaphoreType.DMA,
            pltpu.SemaphoreType.DMA((2,)),
            pltpu.SemaphoreType.DMA((STEPS,)),
        ],
        compiler_params=params(ALL_VMEM),
        cost_estimate=pl.CostEstimate(
            flops=10_000_000, bytes_accessed=20_000_000, transcendentals=0
        ),
        name="gather",
    )(lengths, table, own, other)


def attend(scale, plan, queries, keys):
    sources, requests, wide = queries.shape
    width = keys.shape[0]
    kv = (wide - 128) // 2
    heads = 2 * sources
    return pl.pallas_call(
        functools.partial(attention_kernel, scale),
        out_shape=jax.ShapeDtypeStruct((sources, requests, wide), BF16),
        in_specs=[smem(), anywhere(), anywhere()],
        out_specs=vmem(),
        scratch_shapes=[
            pltpu.VMEM(queries.shape, BF16),
            pltpu.SemaphoreType.DMA,
            pltpu.VMEM((wide // LANES, sources * requests, LANES), F32),
            pltpu.VMEM((requests, heads, width), BF16),
            pltpu.VMEM((GROUPS, heads, 2 * LANES), F32),
            pltpu.VMEM((requests, heads, LANES), F32),
            pltpu.VMEM((requests, heads, LANES), F32),
            pltpu.VMEM((requests, heads, kv), F32),
            pltpu.VMEM(keys.shape, BF16),
            pltpu.SemaphoreType.DMA((STEPS,)),
        ],
        compiler_params=params(58 * MIB),
        cost_estimate=pl.CostEstimate(
            flops=1_200_000_000, bytes_accessed=12_000_000, transcendentals=524_288
        ),
        name="attention",
    )(plan, queries, keys)


def fold(parts, value_up, copies):
    sources, requests, wide = parts.shape
    kv, out = value_up.shape[1:]
    return pl.pallas_call(
        fold_kernel,
        out_shape=jax.ShapeDtypeStruct((copies, requests, 3 * LANES), BF16),
        in_specs=[vmem(), anywhere()],
        out_specs=vmem(),
        scratch_shapes=[pltpu.VMEM((2, kv, out), BF16), pltpu.SemaphoreType.DMA],
        compiler_params=params(),
        name="fold",
    )(parts, value_up)


def merge(parts):
    requests = parts.shape[1]
    return pl.pallas_call(
        merge_kernel,
        out_shape=jax.ShapeDtypeStruct((requests, 4 * LANES), BF16),
        in_specs=[vmem()],
        out_specs=vmem(),
        compiler_params=params(),
        name="merge",
    )(parts)


def local(query_nope, query_rope, key_up, value_up, cache, lengths, table):
    scale = float(query_nope.shape[2] + query_rope.shape[2]) ** -0.5
    rows, cols = lax.axis_size("row"), lax.axis_size("col")
    own = cache.T
    other = lax.ppermute(own, "col", [(i, i ^ 1) for i in range(cols)])
    queries = make_queries(query_nope, query_rope, key_up, rows)
    queries = lax.all_to_all(queries, "row", split_axis=0, concat_axis=0, tiled=True)
    plan, keys = gather(lengths, table, own, other)
    parts = attend(scale, plan, queries, keys)
    parts = lax.all_to_all(parts, "row", split_axis=0, concat_axis=0, tiled=True)
    parts = fold(parts, value_up, cols)
    parts = lax.all_to_all(parts, "col", split_axis=0, concat_axis=0, tiled=True)
    return merge(parts)


def solution(mesh):
    placed = (
        P(None, "row", None),
        P(None, "row", None),
        P("row", None, None),
        P("row", None, None),
        P(("row", "col"), None),
        P(),
        P(),
    )
    return jax.shard_map(
        local, mesh=mesh, in_specs=placed, out_specs=P(None, "row"), check_vma=False
    )
```

```python
import functools

import jax
import jax.numpy as jnp
from jax import lax
from jax.experimental import pallas as pl
from jax.experimental.pallas import tpu as pltpu
from jax.sharding import PartitionSpec as P

PAGE = 64
LANES = 128
EMPTY = -1e30
UNROLL = 4
GROUPS = 40
STEPS = GROUPS // UNROLL
CHUNK = UNROLL * 2 * LANES
MIB = 1024 * 1024
ALL_VMEM = 60 * MIB
ENTRIES = 64
TRASH = 180
PLAN = 1024
SPREAD = 6 * 1024 * 1024
F32 = jnp.float32
BF16 = jnp.bfloat16


def three_terms(value):
    high = value.astype(BF16)
    rest = value - high.astype(F32)
    middle = rest.astype(BF16)
    low = (rest - middle.astype(F32)).astype(BF16)
    return high, middle, low


def stat_lanes(values, rows):
    lane = lax.broadcasted_iota(jnp.int32, (rows, LANES), 1)
    out = jnp.zeros((rows, LANES), F32)
    for head, value in enumerate(values):
        for at, term in enumerate(three_terms(value)):
            out = jnp.where(lane == 64 * head + at, term.astype(F32), out)
    return out


def read_stat(lanes, head):
    at = 64 * head
    return lanes[..., at : at + 1] + lanes[..., at + 1 : at + 2] + lanes[..., at + 2 : at + 3]


def query_kernel(nope_any, rope_any, up_ref, out_ref, nope_ref, rope_ref, up, row, sems, out_sems):
    copies, requests, _ = out_ref.shape
    first = 2 * (lax.axis_index("col") & 1)
    loads = [
        pltpu.make_async_copy(nope_any, nope_ref, sems.at[0]),
        pltpu.make_async_copy(rope_any, rope_ref, sems.at[1]),
        pltpu.make_async_copy(up_ref.at[pl.ds(first, 2)], up, sems.at[2]),
    ]
    for load in loads:
        load.start()

    def head_of(ref, j):
        rows = ref[...].astype(F32)
        head = lax.broadcasted_iota(jnp.int32, rows.shape, 1)
        return jnp.sum(jnp.where(head == first + j, rows, 0.0), axis=1).astype(BF16)

    loads[0].wait()
    nopes = [head_of(nope_ref, j) for j in range(2)]
    loads[1].wait()
    ropes = [head_of(rope_ref, j) for j in range(2)]
    loads[2].wait()
    parts = [
        jnp.dot(nopes[j], up[j], preferred_element_type=F32).astype(BF16) for j in range(2)
    ]
    row[...] = jnp.concatenate(parts + ropes, axis=1)
    stores = [
        pltpu.make_async_copy(row, out_ref.at[k], out_sems.at[k]) for k in range(copies)
    ]
    for store in stores:
        store.start()
    for store in stores:
        store.wait()


def gather_kernel(
    length_ref,
    table_any,
    own_ref,
    other_ref,
    plan_any,
    keys_ref,
    plan_ref,
    table_ref,
    cache,
    keys,
    vec,
    sm,
    count,
    fill,
    sem,
    plan_sem,
    cache_sems,
    out_sems,
):
    loads = [
        pltpu.make_async_copy(own_ref, cache.at[0], cache_sems.at[0]),
        pltpu.make_async_copy(other_ref, cache.at[1], cache_sems.at[1]),
    ]
    copy = pltpu.make_async_copy(table_any, table_ref, sem)
    copy.start()
    for load in loads:
        load.start()
    copy.wait()
    column = lax.axis_index("col")
    core = column & 1
    chip = lax.axis_index("row") * (lax.axis_size("col") // 2) + (column >> 1)
    base = chip * 128
    requests, width = table_ref.shape
    page = lax.broadcasted_iota(jnp.int32, (1, width), 1)
    high = lax.broadcasted_iota(jnp.int32, (8, width), 0)
    low = lax.broadcasted_iota(jnp.int32, (16, width), 0)
    total = jnp.zeros((16, 16), F32)
    for r in range(requests):
        slot = table_ref[r : r + 1, :] - base
        live = jnp.clip(length_ref[r] - page * PAGE, 0, PAGE).astype(F32)
        hit = high == (slot >> 4)
        owner = jnp.where(hit, float(r + 1), 0.0)
        rows = jnp.where(hit, live, 0.0)
        left = jnp.concatenate([owner, rows], axis=0).astype(BF16)
        right = jnp.where(low == (slot & 15), 1.0, 0.0).astype(BF16)
        total = total + lax.dot_general(
            left, right, (((1,), (1,)), ((), ())), preferred_element_type=F32
        )
    vec[:, :16] = total.astype(jnp.int32)
    copy = pltpu.make_async_copy(vec, sm, sem)
    copy.start()
    copy.wait()

    def page_of(i, side):
        s = (2 * i + side + PAGE * core) & 127
        return sm[s >> 4, s & 15], sm[8 + (s >> 4), s & 15]

    for r in range(16):
        count[r] = 0

    def page_of(t):
        s = (t + PAGE * core) & 127
        return sm[s >> 4, s & 15], sm[8 + (s >> 4), s & 15]

    @pl.loop(0, 128, unroll=16)
    def _(t):
        owner, _ = page_of(t)
        count[owner] = count[owner] + 1

    start = jnp.int32(0)
    fill[0] = TRASH
    for r in range(requests):
        fill[r + 1] = 4 * start
        groups = (count[r + 1] + 3) >> 2

        @pl.loop(start, start + groups)
        def _(g):
            plan_ref[8 + g] = r
            for at in range(4):
                plan_ref[ENTRIES + 4 * g + at] = 0

        start = start + groups
    plan_ref[0] = start
    for ahead in range(UNROLL - 1):
        plan_ref[8 + start + ahead] = 0
        for at in range(4):
            plan_ref[ENTRIES + 4 * (start + ahead) + at] = 0

    @pl.loop(0, 128, unroll=8)
    def _(t):
        owner, rows = page_of(t)
        at = fill[owner]
        fill[owner] = at + jnp.where(owner > 0, 1, 0)
        plan_ref[ENTRIES + at] = t + (rows << 8)

    plan_store = pltpu.make_async_copy(plan_ref, plan_any.at[pl.ds(0, PLAN)], plan_sem)
    plan_store.start()
    for load in loads:
        load.wait()
    steps = (plan_ref[0] + UNROLL - 1) // UNROLL
    left_half = lax.broadcasted_iota(jnp.int32, (1, LANES), 1) < PAGE

    def tile_of(entry):
        slot = entry & 127
        at = pl.multiple_of(((slot & 63) >> 1) * LANES, LANES)
        return cache[slot >> 6, :, pl.ds(at, LANES)]

    def turned(tile):
        return jnp.concatenate([tile[:, PAGE:], tile[:, :PAGE]], axis=1)

    def chunk(step):
        return pltpu.make_async_copy(keys.at[step], keys_ref.at[step], out_sems.at[step])

    @pl.loop(0, steps)
    def _(step):
        @pl.loop(0, 2 * UNROLL)
        def _(j):
            entry = ENTRIES + 2 * (2 * UNROLL * step + j)
            first = plan_ref[entry]
            second = plan_ref[entry + 1]
            kind = (first & 1) + 2 * (second & 1)
            at = pl.ds(pl.multiple_of(j * LANES, LANES), LANES)

            @pl.when(kind == 2)
            def _():
                keys[step, :, at] = jnp.where(left_half, tile_of(first), tile_of(second))

            @pl.when(kind == 0)
            def _():
                keys[step, :, at] = jnp.where(left_half, tile_of(first), turned(tile_of(second)))

            @pl.when(kind == 3)
            def _():
                keys[step, :, at] = jnp.where(left_half, turned(tile_of(first)), tile_of(second))

            @pl.when(kind == 1)
            def _():
                keys[step, :, at] = turned(jnp.where(left_half, tile_of(second), tile_of(first)))

        chunk(step).start()

    @pl.loop(0, steps)
    def _(step):
        chunk(step).wait()

    plan_store.wait()


def attention_kernel(
    scale, plan_any, query_any, keys_any, out_ref, plan_ref, plan_sem, query_ref, query_sem, staged, query, scores, top, denom, total, keys_ref, sems
):
    load = pltpu.make_async_copy(query_any, query_ref, query_sem)
    load.start()
    fetch = pltpu.make_async_copy(plan_any.at[pl.ds(0, PLAN)], plan_ref, plan_sem)
    fetch.start()
    fetch.wait()
    groups = plan_ref[0]
    steps = (groups + UNROLL - 1) // UNROLL

    def chunk(step):
        return pltpu.make_async_copy(keys_any.at[step], keys_ref.at[step], sems.at[step])

    @pl.loop(0, steps)
    def _(step):
        chunk(step).start()

    sources, requests, wide = query_ref.shape
    kv = total.shape[2]
    tiles = kv // LANES
    top[...] = jnp.full_like(top, EMPTY)
    denom[...] = jnp.zeros_like(denom)
    total[...] = jnp.zeros_like(total)
    load.wait()
    for t in range(wide // LANES):
        columns = query_ref[:, :, t * LANES : (t + 1) * LANES]
        staged[t] = columns.astype(F32).reshape(sources * requests, LANES)
    for r in range(requests):
        at = pl.ds(r, sources, stride=requests)
        for t in range(tiles):
            columns = slice(t * LANES, (t + 1) * LANES)
            query[r, :sources, columns] = staged[t, at, :].astype(BF16)
            query[r, sources:, columns] = staged[tiles + t, at, :].astype(BF16)
        rows = staged[2 * tiles, at, :].astype(BF16)
        query[r, :sources, kv:] = rows[:, :64]
        query[r, sources:, kv:] = rows[:, 64:]
    lane = lax.broadcasted_iota(jnp.int32, (1, LANES), 1)
    left_half = lane < PAGE
    within = lane & (PAGE - 1)

    def keys(step, u, depth):
        return keys_ref[step, :depth, 2 * LANES * u : 2 * LANES * (u + 1)]

    @pl.loop(0, steps)
    def _(step):
        chunk(step).wait()
        for u in range(UNROLL):
            g = step * UNROLL + u
            r = plan_ref[8 + g]
            score = jnp.dot(query[r], keys(step, u, keys_ref.shape[1]), preferred_element_type=F32)
            halves = []
            for half in range(2):
                rows = jnp.where(
                    left_half,
                    plan_ref[ENTRIES + 4 * g + 2 * half] >> 8,
                    plan_ref[ENTRIES + 4 * g + 2 * half + 1] >> 8,
                )
                part = score[:, half * LANES : (half + 1) * LANES]
                part = jnp.where(within < rows, part, EMPTY)
                scores[g, :, half * LANES : (half + 1) * LANES] = part
                halves.append(part)
            top[r] = jnp.maximum(top[r], jnp.maximum(*halves))

    for r in range(requests):
        top[r] = jnp.broadcast_to(jnp.max(top[r], axis=1, keepdims=True), top.shape[1:])

    @pl.loop(0, steps)
    def _(step):
        for u in range(UNROLL):
            g = step * UNROLL + u
            r = plan_ref[8 + g]
            level = top[r]
            live = jnp.where(g < groups, 1.0, 0.0)
            halves = []
            for half in range(2):
                part = scores[g, :, half * LANES : (half + 1) * LANES]
                halves.append((jnp.exp((part - level) * scale) * live).astype(BF16))
            denom[r] = denom[r] + halves[0].astype(F32) + halves[1].astype(F32)
            total[r] = total[r] + lax.dot_general(
                jnp.concatenate(halves, axis=1),
                keys(step, u, kv),
                (((1,), (1,)), ((), ())),
                preferred_element_type=F32,
            )

    for r in range(requests):
        sums = jnp.sum(denom[r], axis=1, keepdims=True)
        some = sums > 0.0
        safe = jnp.where(some, sums, 1.0)
        level = jnp.where(some, top[r][:, :1] * scale + jnp.log(safe), EMPTY)
        rows = total[r] * (1.0 / safe)
        at = pl.ds(r, sources, stride=requests)
        for t in range(tiles):
            columns = slice(t * LANES, (t + 1) * LANES)
            staged[t, at, :] = rows[:sources, columns]
            staged[tiles + t, at, :] = rows[sources:, columns]
        staged[2 * tiles, at, :] = stat_lanes([level[:sources], level[sources:]], sources)
    for t in range(wide // LANES):
        columns = slice(t * LANES, (t + 1) * LANES)
        out_ref[:, :, columns] = staged[t].reshape(sources, requests, LANES).astype(BF16)


def fold_kernel(part_ref, up_any, out_ref, up_ref, sem):
    first = 2 * (lax.axis_index("col") & 1)
    load = pltpu.make_async_copy(up_any.at[pl.ds(first, 2)], up_ref, sem)
    load.start()
    sources, requests, wide = part_ref.shape
    kv = up_ref.shape[1]
    stats = part_ref[:, :, 2 * kv :].astype(F32)
    outputs, levels = [], []
    for j in range(2):
        level = read_stat(stats, j)
        peak = jnp.max(level, axis=0)
        weight = jnp.exp(level - peak[None])
        norm = jnp.sum(weight, axis=0)
        rows = part_ref[:, :, j * kv : (j + 1) * kv].astype(F32)
        rows = jnp.sum(rows * weight, axis=0) / norm
        if j == 0:
            load.wait()
        outputs.append(jnp.dot(rows.astype(BF16), up_ref[j], preferred_element_type=F32))
        levels.append(peak + jnp.log(norm))
    block = jnp.concatenate(outputs + [stat_lanes(levels, requests)], axis=1).astype(BF16)
    for k in range(out_ref.shape[0]):
        out_ref[k] = block


def merge_kernel(part_ref, out_ref):
    width = 2 * LANES
    both = part_ref[...].astype(F32)
    both = both.reshape(both.shape[0] // 2, 2, *both.shape[1:])
    for core in range(2):
        parts = both[:, core]
        stats = parts[:, :, width:]
        for j in range(2):
            level = read_stat(stats, j)
            weight = jnp.exp(level - jnp.max(level, axis=0)[None])
            rows = jnp.sum(parts[:, :, j * LANES : (j + 1) * LANES] * weight, axis=0)
            rows = rows / jnp.sum(weight, axis=0)
            at = (2 * core + j) * LANES
            out_ref[:, at : at + LANES] = rows.astype(BF16)


def vmem():
    return pl.BlockSpec(memory_space=pltpu.VMEM)


def smem():
    return pl.BlockSpec(memory_space=pltpu.SMEM)


def anywhere():
    return pl.BlockSpec(memory_space=pl.ANY)


def params(limit=32 * MIB):
    return pltpu.CompilerParams(vmem_limit_bytes=limit)


def make_queries(nope, rope, key_up, copies):
    requests, heads, width = nope.shape
    kv = key_up.shape[2]
    wide = 2 * kv + 2 * rope.shape[2]
    return pl.pallas_call(
        query_kernel,
        out_shape=jax.ShapeDtypeStruct((copies, requests, wide), BF16),
        in_specs=[anywhere(), anywhere(), anywhere()],
        out_specs=anywhere(),
        scratch_shapes=[
            pltpu.VMEM(nope.shape, BF16),
            pltpu.VMEM(rope.shape, BF16),
            pltpu.VMEM((2, width, kv), BF16),
            pltpu.VMEM((requests, wide), BF16),
            pltpu.SemaphoreType.DMA((3,)),
            pltpu.SemaphoreType.DMA((copies,)),
        ],
        compiler_params=params(ALL_VMEM),
        name="queries",
    )(nope, rope, key_up)


def gather(lengths, table, own, other):
    width, tokens = own.shape
    return pl.pallas_call(
        gather_kernel,
        out_shape=(
            jax.ShapeDtypeStruct((SPREAD,), jnp.int32),
            jax.ShapeDtypeStruct((2 * STEPS, width, CHUNK), BF16),
        ),
        in_specs=[smem(), anywhere(), anywhere(), anywhere()],
        out_specs=(anywhere(), anywhere()),
        scratch_shapes=[
            pltpu.SMEM((PLAN,), jnp.int32),
            pltpu.VMEM(table.shape, jnp.int32),
            pltpu.VMEM((2, width, tokens), BF16),
            pltpu.VMEM((STEPS, width, CHUNK), BF16),
            pltpu.VMEM((16, LANES), jnp.int32),
            pltpu.SMEM((16, LANES), jnp.int32),
            pltpu.SMEM((16,), jnp.int32),
            pltpu.SMEM((16,), jnp.int32),
            pltpu.SemaphoreType.DMA,
            pltpu.SemaphoreType.DMA,
            pltpu.SemaphoreType.DMA((2,)),
            pltpu.SemaphoreType.DMA((STEPS,)),
        ],
        compiler_params=params(ALL_VMEM),
        cost_estimate=pl.CostEstimate(
            flops=10_000_000, bytes_accessed=20_000_000, transcendentals=0
        ),
        name="gather",
    )(lengths, table, own, other)


def attend(scale, plan, queries, keys):
    sources, requests, wide = queries.shape
    width = keys.shape[1]
    kv = (wide - 128) // 2
    heads = 2 * sources
    return pl.pallas_call(
        functools.partial(attention_kernel, scale),
        out_shape=jax.ShapeDtypeStruct((sources, requests, wide), BF16),
        in_specs=[anywhere(), anywhere(), anywhere()],
        out_specs=vmem(),
        scratch_shapes=[
            pltpu.SMEM((PLAN,), jnp.int32),
            pltpu.SemaphoreType.DMA,
            pltpu.VMEM(queries.shape, BF16),
            pltpu.SemaphoreType.DMA,
            pltpu.VMEM((wide // LANES, sources * requests, LANES), F32),
            pltpu.VMEM((requests, heads, width), BF16),
            pltpu.VMEM((GROUPS, heads, 2 * LANES), F32),
            pltpu.VMEM((requests, heads, LANES), F32),
            pltpu.VMEM((requests, heads, LANES), F32),
            pltpu.VMEM((requests, heads, kv), F32),
            pltpu.VMEM((STEPS, width, CHUNK), BF16),
            pltpu.SemaphoreType.DMA((STEPS,)),
        ],
        compiler_params=params(40 * MIB),
        cost_estimate=pl.CostEstimate(
            flops=1_200_000_000, bytes_accessed=12_000_000, transcendentals=524_288
        ),
        name="attention",
    )(plan, queries, keys)


def fold(parts, value_up, copies):
    sources, requests, wide = parts.shape
    kv, out = value_up.shape[1:]
    return pl.pallas_call(
        fold_kernel,
        out_shape=jax.ShapeDtypeStruct((copies, requests, 3 * LANES), BF16),
        in_specs=[vmem(), anywhere()],
        out_specs=vmem(),
        scratch_shapes=[pltpu.VMEM((2, kv, out), BF16), pltpu.SemaphoreType.DMA],
        compiler_params=params(),
        name="fold",
    )(parts, value_up)


def merge(parts):
    requests = parts.shape[1]
    return pl.pallas_call(
        merge_kernel,
        out_shape=jax.ShapeDtypeStruct((requests, 4 * LANES), BF16),
        in_specs=[vmem()],
        out_specs=vmem(),
        compiler_params=params(),
        name="merge",
    )(parts)


def local(query_nope, query_rope, key_up, value_up, cache, lengths, table):
    scale = float(query_nope.shape[2] + query_rope.shape[2]) ** -0.5
    rows, cols = lax.axis_size("row"), lax.axis_size("col")
    own = cache.T
    other = lax.ppermute(own, "col", [(i, i ^ 1) for i in range(cols)])
    queries = make_queries(query_nope, query_rope, key_up, rows)
    queries = lax.all_to_all(queries, "row", split_axis=0, concat_axis=0, tiled=True)
    plan, keys = gather(lengths, table, own, other)
    parts = attend(scale, plan, queries, keys)
    parts = lax.all_to_all(parts, "row", split_axis=0, concat_axis=0, tiled=True)
    parts = fold(parts, value_up, cols)
    parts = lax.all_to_all(parts, "col", split_axis=0, concat_axis=0, tiled=True)
    return merge(parts)


def solution(mesh):
    placed = (
        P(None, "row", None),
        P(None, "row", None),
        P("row", None, None),
        P("row", None, None),
        P(("row", "col"), None),
        P(),
        P(),
    )
    return jax.shard_map(
        local, mesh=mesh, in_specs=placed, out_specs=P(None, "row"), check_vma=False
    )
```

```python
import functools

import jax
import jax.numpy as jnp
from jax import lax
from jax.experimental import pallas as pl
from jax.experimental.pallas import tpu as pltpu
from jax.sharding import PartitionSpec as P

PAGE = 64
LANES = 128
EMPTY = -1e30
UNROLL = 4
GROUPS = 40
STEPS = GROUPS // UNROLL
CHUNK = UNROLL * 2 * LANES
MIB = 1024 * 1024
ALL_VMEM = 60 * MIB
ENTRIES = 64
TRASH = 180
PLAN = 1024
EARLY = 3
SPREAD = 6 * 1024 * 1024
F32 = jnp.float32
BF16 = jnp.bfloat16


def three_terms(value):
    high = value.astype(BF16)
    rest = value - high.astype(F32)
    middle = rest.astype(BF16)
    low = (rest - middle.astype(F32)).astype(BF16)
    return high, middle, low


def stat_lanes(values, rows):
    lane = lax.broadcasted_iota(jnp.int32, (rows, LANES), 1)
    out = jnp.zeros((rows, LANES), F32)
    for head, value in enumerate(values):
        for at, term in enumerate(three_terms(value)):
            out = jnp.where(lane == 64 * head + at, term.astype(F32), out)
    return out


def read_stat(lanes, head):
    at = 64 * head
    return lanes[..., at : at + 1] + lanes[..., at + 1 : at + 2] + lanes[..., at + 2 : at + 3]


def query_kernel(nope_any, rope_any, up_ref, out_ref, nope_ref, rope_ref, up, row, sems, out_sems):
    copies, requests, _ = out_ref.shape
    first = 2 * (lax.axis_index("col") & 1)
    loads = [
        pltpu.make_async_copy(nope_any, nope_ref, sems.at[0]),
        pltpu.make_async_copy(rope_any, rope_ref, sems.at[1]),
        pltpu.make_async_copy(up_ref.at[pl.ds(first, 2)], up, sems.at[2]),
    ]
    for load in loads:
        load.start()

    def head_of(ref, j):
        rows = ref[...].astype(F32)
        head = lax.broadcasted_iota(jnp.int32, rows.shape, 1)
        return jnp.sum(jnp.where(head == first + j, rows, 0.0), axis=1).astype(BF16)

    loads[0].wait()
    nopes = [head_of(nope_ref, j) for j in range(2)]
    loads[1].wait()
    ropes = [head_of(rope_ref, j) for j in range(2)]
    loads[2].wait()
    parts = [
        jnp.dot(nopes[j], up[j], preferred_element_type=F32).astype(BF16) for j in range(2)
    ]
    row[...] = jnp.concatenate(parts + ropes, axis=1)
    stores = [
        pltpu.make_async_copy(row, out_ref.at[k], out_sems.at[k]) for k in range(copies)
    ]
    for store in stores:
        store.start()
    for store in stores:
        store.wait()


def gather_kernel(
    length_ref,
    table_any,
    own_ref,
    other_ref,
    plan_any,
    keys_ref,
    plan_ref,
    table_ref,
    cache,
    keys,
    vec,
    sm,
    count,
    fill,
    sem,
    plan_sem,
    cache_sems,
    out_sems,
):
    loads = [
        pltpu.make_async_copy(own_ref, cache.at[0], cache_sems.at[0]),
        pltpu.make_async_copy(other_ref, cache.at[1], cache_sems.at[1]),
    ]
    copy = pltpu.make_async_copy(table_any, table_ref, sem)
    copy.start()
    for load in loads:
        load.start()
    copy.wait()
    column = lax.axis_index("col")
    core = column & 1
    chip = lax.axis_index("row") * (lax.axis_size("col") // 2) + (column >> 1)
    base = chip * 128
    requests, width = table_ref.shape
    page = lax.broadcasted_iota(jnp.int32, (1, width), 1)
    high = lax.broadcasted_iota(jnp.int32, (8, width), 0)
    low = lax.broadcasted_iota(jnp.int32, (16, width), 0)
    total = jnp.zeros((16, 16), F32)
    for r in range(requests):
        slot = table_ref[r : r + 1, :] - base
        live = jnp.clip(length_ref[r] - page * PAGE, 0, PAGE).astype(F32)
        hit = high == (slot >> 4)
        owner = jnp.where(hit, float(r + 1), 0.0)
        rows = jnp.where(hit, live, 0.0)
        left = jnp.concatenate([owner, rows], axis=0).astype(BF16)
        right = jnp.where(low == (slot & 15), 1.0, 0.0).astype(BF16)
        total = total + lax.dot_general(
            left, right, (((1,), (1,)), ((), ())), preferred_element_type=F32
        )
    vec[:, :16] = total.astype(jnp.int32)
    copy = pltpu.make_async_copy(vec, sm, sem)
    copy.start()
    copy.wait()

    def page_of(i, side):
        s = (2 * i + side + PAGE * core) & 127
        return sm[s >> 4, s & 15], sm[8 + (s >> 4), s & 15]

    for r in range(16):
        count[r] = 0

    def page_of(t):
        s = (t + PAGE * core) & 127
        return sm[s >> 4, s & 15], sm[8 + (s >> 4), s & 15]

    @pl.loop(0, 128, unroll=16)
    def _(t):
        owner, _ = page_of(t)
        count[owner] = count[owner] + 1

    start = jnp.int32(0)
    fill[0] = TRASH
    for r in range(requests):
        fill[r + 1] = 4 * start
        groups = (count[r + 1] + 3) >> 2

        @pl.loop(start, start + groups)
        def _(g):
            plan_ref[8 + g] = r
            for at in range(4):
                plan_ref[ENTRIES + 4 * g + at] = 0

        start = start + groups
    plan_ref[0] = start
    for ahead in range(UNROLL - 1):
        plan_ref[8 + start + ahead] = 0
        for at in range(4):
            plan_ref[ENTRIES + 4 * (start + ahead) + at] = 0

    @pl.loop(0, 128, unroll=8)
    def _(t):
        owner, rows = page_of(t)
        at = fill[owner]
        fill[owner] = at + jnp.where(owner > 0, 1, 0)
        plan_ref[ENTRIES + at] = t + (rows << 8)

    plan_store = pltpu.make_async_copy(plan_ref, plan_any.at[pl.ds(0, PLAN)], plan_sem)
    plan_store.start()
    for load in loads:
        load.wait()
    steps = (plan_ref[0] + UNROLL - 1) // UNROLL
    left_half = lax.broadcasted_iota(jnp.int32, (1, LANES), 1) < PAGE

    def tile_of(entry):
        slot = entry & 127
        at = pl.multiple_of(((slot & 63) >> 1) * LANES, LANES)
        return cache[slot >> 6, :, pl.ds(at, LANES)]

    def turned(tile):
        return jnp.concatenate([tile[:, PAGE:], tile[:, :PAGE]], axis=1)

    def chunk(step):
        return pltpu.make_async_copy(keys.at[step], keys_ref.at[step], out_sems.at[step])

    @pl.loop(0, steps)
    def _(step):
        @pl.loop(0, 2 * UNROLL)
        def _(j):
            entry = ENTRIES + 2 * (2 * UNROLL * step + j)
            first = plan_ref[entry]
            second = plan_ref[entry + 1]
            kind = (first & 1) + 2 * (second & 1)
            at = pl.ds(pl.multiple_of(j * LANES, LANES), LANES)

            @pl.when(kind == 2)
            def _():
                keys[step, :, at] = jnp.where(left_half, tile_of(first), tile_of(second))

            @pl.when(kind == 0)
            def _():
                keys[step, :, at] = jnp.where(left_half, tile_of(first), turned(tile_of(second)))

            @pl.when(kind == 3)
            def _():
                keys[step, :, at] = jnp.where(left_half, turned(tile_of(first)), tile_of(second))

            @pl.when(kind == 1)
            def _():
                keys[step, :, at] = turned(jnp.where(left_half, tile_of(second), tile_of(first)))

        chunk(step).start()

    @pl.loop(0, steps)
    def _(step):
        chunk(step).wait()

    plan_store.wait()


def attention_kernel(
    scale, plan_any, query_any, keys_any, out_ref, plan_ref, plan_sem, query_ref, query_sem, staged, query, scores, top, denom, total, keys_ref, sems
):
    load = pltpu.make_async_copy(query_any, query_ref, query_sem)
    load.start()
    fetch = pltpu.make_async_copy(plan_any.at[pl.ds(0, PLAN)], plan_ref, plan_sem)
    fetch.start()

    def chunk(step):
        return pltpu.make_async_copy(keys_any.at[step], keys_ref.at[step], sems.at[step])

    sources, requests, wide = query_ref.shape
    kv = total.shape[2]
    tiles = kv // LANES
    for step in range(EARLY):
        chunk(step).start()
    fetch.wait()
    groups = plan_ref[0]
    steps = (groups + UNROLL - 1) // UNROLL

    @pl.loop(EARLY, jnp.maximum(steps, EARLY))
    def _(step):
        chunk(step).start()

    top[...] = jnp.full_like(top, EMPTY)
    denom[...] = jnp.zeros_like(denom)
    total[...] = jnp.zeros_like(total)
    load.wait()
    for t in range(wide // LANES):
        columns = query_ref[:, :, t * LANES : (t + 1) * LANES]
        staged[t] = columns.astype(F32).reshape(sources * requests, LANES)
    for r in range(requests):
        at = pl.ds(r, sources, stride=requests)
        for t in range(tiles):
            columns = slice(t * LANES, (t + 1) * LANES)
            query[r, :sources, columns] = staged[t, at, :].astype(BF16)
            query[r, sources:, columns] = staged[tiles + t, at, :].astype(BF16)
        rows = staged[2 * tiles, at, :].astype(BF16)
        query[r, :sources, kv:] = rows[:, :64]
        query[r, sources:, kv:] = rows[:, 64:]
    lane = lax.broadcasted_iota(jnp.int32, (1, LANES), 1)
    left_half = lane < PAGE
    within = lane & (PAGE - 1)

    def keys(step, u, depth):
        return keys_ref[step, :depth, 2 * LANES * u : 2 * LANES * (u + 1)]

    @pl.loop(0, steps)
    def _(step):
        chunk(step).wait()
        for u in range(UNROLL):
            g = step * UNROLL + u
            r = plan_ref[8 + g]
            score = jnp.dot(query[r], keys(step, u, keys_ref.shape[1]), preferred_element_type=F32)
            halves = []
            for half in range(2):
                rows = jnp.where(
                    left_half,
                    plan_ref[ENTRIES + 4 * g + 2 * half] >> 8,
                    plan_ref[ENTRIES + 4 * g + 2 * half + 1] >> 8,
                )
                part = score[:, half * LANES : (half + 1) * LANES]
                part = jnp.where(within < rows, part, EMPTY)
                scores[g, :, half * LANES : (half + 1) * LANES] = part
                halves.append(part)
            top[r] = jnp.maximum(top[r], jnp.maximum(*halves))

    @pl.loop(jnp.minimum(steps, EARLY), EARLY)
    def _(step):
        chunk(step).wait()

    for r in range(requests):
        top[r] = jnp.broadcast_to(jnp.max(top[r], axis=1, keepdims=True), top.shape[1:])

    @pl.loop(0, steps)
    def _(step):
        for u in range(UNROLL):
            g = step * UNROLL + u
            r = plan_ref[8 + g]
            level = top[r]
            live = jnp.where(g < groups, 1.0, 0.0)
            halves = []
            for half in range(2):
                part = scores[g, :, half * LANES : (half + 1) * LANES]
                halves.append((jnp.exp((part - level) * scale) * live).astype(BF16))
            denom[r] = denom[r] + halves[0].astype(F32) + halves[1].astype(F32)
            total[r] = total[r] + lax.dot_general(
                jnp.concatenate(halves, axis=1),
                keys(step, u, kv),
                (((1,), (1,)), ((), ())),
                preferred_element_type=F32,
            )

    for r in range(requests):
        sums = jnp.sum(denom[r], axis=1, keepdims=True)
        some = sums > 0.0
        safe = jnp.where(some, sums, 1.0)
        level = jnp.where(some, top[r][:, :1] * scale + jnp.log(safe), EMPTY)
        rows = total[r] * (1.0 / safe)
        at = pl.ds(r, sources, stride=requests)
        for t in range(tiles):
            columns = slice(t * LANES, (t + 1) * LANES)
            staged[t, at, :] = rows[:sources, columns]
            staged[tiles + t, at, :] = rows[sources:, columns]
        staged[2 * tiles, at, :] = stat_lanes([level[:sources], level[sources:]], sources)
    for t in range(wide // LANES):
        columns = slice(t * LANES, (t + 1) * LANES)
        out_ref[:, :, columns] = staged[t].reshape(sources, requests, LANES).astype(BF16)


def fold_kernel(part_ref, up_any, out_ref, up_ref, sem):
    first = 2 * (lax.axis_index("col") & 1)
    load = pltpu.make_async_copy(up_any.at[pl.ds(first, 2)], up_ref, sem)
    load.start()
    sources, requests, wide = part_ref.shape
    kv = up_ref.shape[1]
    stats = part_ref[:, :, 2 * kv :].astype(F32)
    outputs, levels = [], []
    for j in range(2):
        level = read_stat(stats, j)
        peak = jnp.max(level, axis=0)
        weight = jnp.exp(level - peak[None])
        norm = jnp.sum(weight, axis=0)
        rows = part_ref[:, :, j * kv : (j + 1) * kv].astype(F32)
        rows = jnp.sum(rows * weight, axis=0) / norm
        if j == 0:
            load.wait()
        outputs.append(jnp.dot(rows.astype(BF16), up_ref[j], preferred_element_type=F32))
        levels.append(peak + jnp.log(norm))
    block = jnp.concatenate(outputs + [stat_lanes(levels, requests)], axis=1).astype(BF16)
    for k in range(out_ref.shape[0]):
        out_ref[k] = block


def merge_kernel(part_ref, out_ref):
    width = 2 * LANES
    both = part_ref[...].astype(F32)
    both = both.reshape(both.shape[0] // 2, 2, *both.shape[1:])
    for core in range(2):
        parts = both[:, core]
        stats = parts[:, :, width:]
        for j in range(2):
            level = read_stat(stats, j)
            weight = jnp.exp(level - jnp.max(level, axis=0)[None])
            rows = jnp.sum(parts[:, :, j * LANES : (j + 1) * LANES] * weight, axis=0)
            rows = rows / jnp.sum(weight, axis=0)
            at = (2 * core + j) * LANES
            out_ref[:, at : at + LANES] = rows.astype(BF16)


def vmem():
    return pl.BlockSpec(memory_space=pltpu.VMEM)


def smem():
    return pl.BlockSpec(memory_space=pltpu.SMEM)


def anywhere():
    return pl.BlockSpec(memory_space=pl.ANY)


def params(limit=32 * MIB):
    return pltpu.CompilerParams(vmem_limit_bytes=limit)


def make_queries(nope, rope, key_up, copies):
    requests, heads, width = nope.shape
    kv = key_up.shape[2]
    wide = 2 * kv + 2 * rope.shape[2]
    return pl.pallas_call(
        query_kernel,
        out_shape=jax.ShapeDtypeStruct((copies, requests, wide), BF16),
        in_specs=[anywhere(), anywhere(), anywhere()],
        out_specs=anywhere(),
        scratch_shapes=[
            pltpu.VMEM(nope.shape, BF16),
            pltpu.VMEM(rope.shape, BF16),
            pltpu.VMEM((2, width, kv), BF16),
            pltpu.VMEM((requests, wide), BF16),
            pltpu.SemaphoreType.DMA((3,)),
            pltpu.SemaphoreType.DMA((copies,)),
        ],
        compiler_params=params(ALL_VMEM),
        name="queries",
    )(nope, rope, key_up)


def gather(lengths, table, own, other):
    width, tokens = own.shape
    return pl.pallas_call(
        gather_kernel,
        out_shape=(
            jax.ShapeDtypeStruct((SPREAD,), jnp.int32),
            jax.ShapeDtypeStruct((2 * STEPS, width, CHUNK), BF16),
        ),
        in_specs=[smem(), anywhere(), anywhere(), anywhere()],
        out_specs=(anywhere(), anywhere()),
        scratch_shapes=[
            pltpu.SMEM((PLAN,), jnp.int32),
            pltpu.VMEM(table.shape, jnp.int32),
            pltpu.VMEM((2, width, tokens), BF16),
            pltpu.VMEM((STEPS, width, CHUNK), BF16),
            pltpu.VMEM((16, LANES), jnp.int32),
            pltpu.SMEM((16, LANES), jnp.int32),
            pltpu.SMEM((16,), jnp.int32),
            pltpu.SMEM((16,), jnp.int32),
            pltpu.SemaphoreType.DMA,
            pltpu.SemaphoreType.DMA,
            pltpu.SemaphoreType.DMA((2,)),
            pltpu.SemaphoreType.DMA((STEPS,)),
        ],
        compiler_params=params(ALL_VMEM),
        cost_estimate=pl.CostEstimate(
            flops=10_000_000, bytes_accessed=20_000_000, transcendentals=0
        ),
        name="gather",
    )(lengths, table, own, other)


def attend(scale, plan, queries, keys):
    sources, requests, wide = queries.shape
    width = keys.shape[1]
    kv = (wide - 128) // 2
    heads = 2 * sources
    return pl.pallas_call(
        functools.partial(attention_kernel, scale),
        out_shape=jax.ShapeDtypeStruct((sources, requests, wide), BF16),
        in_specs=[anywhere(), anywhere(), anywhere()],
        out_specs=vmem(),
        scratch_shapes=[
            pltpu.SMEM((PLAN,), jnp.int32),
            pltpu.SemaphoreType.DMA,
            pltpu.VMEM(queries.shape, BF16),
            pltpu.SemaphoreType.DMA,
            pltpu.VMEM((wide // LANES, sources * requests, LANES), F32),
            pltpu.VMEM((requests, heads, width), BF16),
            pltpu.VMEM((GROUPS, heads, 2 * LANES), F32),
            pltpu.VMEM((requests, heads, LANES), F32),
            pltpu.VMEM((requests, heads, LANES), F32),
            pltpu.VMEM((requests, heads, kv), F32),
            pltpu.VMEM((STEPS, width, CHUNK), BF16),
            pltpu.SemaphoreType.DMA((STEPS,)),
        ],
        compiler_params=params(40 * MIB),
        cost_estimate=pl.CostEstimate(
            flops=1_200_000_000, bytes_accessed=12_000_000, transcendentals=524_288
        ),
        name="attention",
    )(plan, queries, keys)


def fold(parts, value_up, copies):
    sources, requests, wide = parts.shape
    kv, out = value_up.shape[1:]
    return pl.pallas_call(
        fold_kernel,
        out_shape=jax.ShapeDtypeStruct((copies, requests, 3 * LANES), BF16),
        in_specs=[vmem(), anywhere()],
        out_specs=vmem(),
        scratch_shapes=[pltpu.VMEM((2, kv, out), BF16), pltpu.SemaphoreType.DMA],
        compiler_params=params(),
        name="fold",
    )(parts, value_up)


def merge(parts):
    requests = parts.shape[1]
    return pl.pallas_call(
        merge_kernel,
        out_shape=jax.ShapeDtypeStruct((requests, 4 * LANES), BF16),
        in_specs=[vmem()],
        out_specs=vmem(),
        compiler_params=params(),
        name="merge",
    )(parts)


def local(query_nope, query_rope, key_up, value_up, cache, lengths, table):
    scale = float(query_nope.shape[2] + query_rope.shape[2]) ** -0.5
    rows, cols = lax.axis_size("row"), lax.axis_size("col")
    own = cache.T
    other = lax.ppermute(own, "col", [(i, i ^ 1) for i in range(cols)])
    queries = make_queries(query_nope, query_rope, key_up, rows)
    queries = lax.all_to_all(queries, "row", split_axis=0, concat_axis=0, tiled=True)
    plan, keys = gather(lengths, table, own, other)
    parts = attend(scale, plan, queries, keys)
    parts = lax.all_to_all(parts, "row", split_axis=0, concat_axis=0, tiled=True)
    parts = fold(parts, value_up, cols)
    parts = lax.all_to_all(parts, "col", split_axis=0, concat_axis=0, tiled=True)
    return merge(parts)


def solution(mesh):
    placed = (
        P(None, "row", None),
        P(None, "row", None),
        P("row", None, None),
        P("row", None, None),
        P(("row", "col"), None),
        P(),
        P(),
    )
    return jax.shard_map(
        local, mesh=mesh, in_specs=placed, out_specs=P(None, "row"), check_vma=False
    )
```

```python
import functools

import jax
import jax.numpy as jnp
from jax import lax
from jax.experimental import pallas as pl
from jax.experimental.pallas import tpu as pltpu
from jax.sharding import PartitionSpec as P

PAGE = 64
LANES = 128
EMPTY = -1e30
UNROLL = 4
GROUPS = 36
STEPS = GROUPS // UNROLL
CHUNK = UNROLL * 2 * LANES
MIB = 1024 * 1024
ALL_VMEM = 60 * MIB
ENTRIES = 128
TRASH = 180
PLAN = 1024
SPARE = 15
EARLY = 3
SPREAD = 6 * 1024 * 1024
F32 = jnp.float32
BF16 = jnp.bfloat16


def three_terms(value):
    high = value.astype(BF16)
    rest = value - high.astype(F32)
    middle = rest.astype(BF16)
    low = (rest - middle.astype(F32)).astype(BF16)
    return high, middle, low


def stat_lanes(values, rows):
    lane = lax.broadcasted_iota(jnp.int32, (rows, LANES), 1)
    out = jnp.zeros((rows, LANES), F32)
    for head, value in enumerate(values):
        for at, term in enumerate(three_terms(value)):
            out = jnp.where(lane == 64 * head + at, term.astype(F32), out)
    return out


def read_stat(lanes, head):
    at = 64 * head
    return lanes[..., at : at + 1] + lanes[..., at + 1 : at + 2] + lanes[..., at + 2 : at + 3]


def query_kernel(nope_any, rope_any, up_ref, out_ref, nope_ref, rope_ref, up, row, sems, out_sems):
    copies, requests, _ = out_ref.shape
    first = 2 * (lax.axis_index("col") & 1)
    loads = [
        pltpu.make_async_copy(nope_any, nope_ref, sems.at[0]),
        pltpu.make_async_copy(rope_any, rope_ref, sems.at[1]),
        pltpu.make_async_copy(up_ref.at[pl.ds(first, 2)], up, sems.at[2]),
    ]
    for load in loads:
        load.start()

    def head_of(ref, j):
        rows = ref[...].astype(F32)
        head = lax.broadcasted_iota(jnp.int32, rows.shape, 1)
        return jnp.sum(jnp.where(head == first + j, rows, 0.0), axis=1).astype(BF16)

    loads[0].wait()
    nopes = [head_of(nope_ref, j) for j in range(2)]
    loads[1].wait()
    ropes = [head_of(rope_ref, j) for j in range(2)]
    loads[2].wait()
    parts = [
        jnp.dot(nopes[j], up[j], preferred_element_type=F32).astype(BF16) for j in range(2)
    ]
    row[...] = jnp.concatenate(parts + ropes, axis=1)
    stores = [
        pltpu.make_async_copy(row, out_ref.at[k], out_sems.at[k]) for k in range(copies)
    ]
    for store in stores:
        store.start()
    for store in stores:
        store.wait()


def gather_kernel(
    length_ref,
    table_any,
    own_ref,
    other_ref,
    plan_any,
    keys_ref,
    plan_ref,
    table_ref,
    cache,
    keys,
    vec,
    sm,
    count,
    fill,
    sem,
    plan_sem,
    cache_sems,
    out_sems,
):
    loads = [
        pltpu.make_async_copy(own_ref, cache.at[0], cache_sems.at[0]),
        pltpu.make_async_copy(other_ref, cache.at[1], cache_sems.at[1]),
    ]
    copy = pltpu.make_async_copy(table_any, table_ref, sem)
    copy.start()
    for load in loads:
        load.start()
    copy.wait()
    column = lax.axis_index("col")
    core = column & 1
    chip = lax.axis_index("row") * (lax.axis_size("col") // 2) + (column >> 1)
    base = chip * 128
    requests, width = table_ref.shape
    page = lax.broadcasted_iota(jnp.int32, (1, width), 1)
    high = lax.broadcasted_iota(jnp.int32, (8, width), 0)
    low = lax.broadcasted_iota(jnp.int32, (16, width), 0)
    total = jnp.zeros((16, 16), F32)
    for r in range(requests):
        slot = table_ref[r : r + 1, :] - base
        live = jnp.clip(length_ref[r] - page * PAGE, 0, PAGE).astype(F32)
        hit = high == (slot >> 4)
        owner = jnp.where(hit, float(r + 1), 0.0)
        rows = jnp.where(hit, live, 0.0)
        left = jnp.concatenate([owner, rows], axis=0).astype(BF16)
        right = jnp.where(low == (slot & 15), 1.0, 0.0).astype(BF16)
        total = total + lax.dot_general(
            left, right, (((1,), (1,)), ((), ())), preferred_element_type=F32
        )
    vec[:, :16] = total.astype(jnp.int32)
    copy = pltpu.make_async_copy(vec, sm, sem)
    copy.start()
    copy.wait()

    def page_of(i, side):
        s = (2 * i + side + PAGE * core) & 127
        return sm[s >> 4, s & 15], sm[8 + (s >> 4), s & 15]

    for r in range(16):
        count[r] = 0

    def page_of(t):
        s = (t + PAGE * core) & 127
        return sm[s >> 4, s & 15], sm[8 + (s >> 4), s & 15]

    @pl.loop(0, 128, unroll=16)
    def _(t):
        owner, _ = page_of(t)
        count[owner] = count[owner] + 1

    start = jnp.int32(0)
    fill[0] = TRASH
    for r in range(requests):
        fill[r + 1] = 2 * start
        tiles = (count[r + 1] + 1) >> 1

        @pl.loop(start, start + tiles)
        def _(t):
            plan_ref[8 + t] = r

        @pl.when(tiles > 0)
        def _():
            plan_ref[ENTRIES + 2 * (start + tiles) - 1] = 0

        start = start + tiles
    plan_ref[0] = start
    for ahead in range(2 * UNROLL - 1):
        plan_ref[8 + start + ahead] = 0
        for at in range(2):
            plan_ref[ENTRIES + 2 * (start + ahead) + at] = 0

    @pl.loop(0, 128, unroll=8)
    def _(t):
        owner, rows = page_of(t)
        at = fill[owner]
        fill[owner] = at + jnp.where(owner > 0, 1, 0)
        plan_ref[ENTRIES + at] = t + (rows << 8)

    plan_store = pltpu.make_async_copy(plan_ref, plan_any.at[pl.ds(0, PLAN)], plan_sem)
    plan_store.start()
    for load in loads:
        load.wait()
    steps = (plan_ref[0] + 2 * UNROLL - 1) // (2 * UNROLL)
    left_half = lax.broadcasted_iota(jnp.int32, (1, LANES), 1) < PAGE

    def tile_of(entry):
        slot = entry & 127
        at = pl.multiple_of(((slot & 63) >> 1) * LANES, LANES)
        return cache[slot >> 6, :, pl.ds(at, LANES)]

    def turned(tile):
        return jnp.concatenate([tile[:, PAGE:], tile[:, :PAGE]], axis=1)

    def chunk(step):
        return pltpu.make_async_copy(keys.at[step], keys_ref.at[step], out_sems.at[step])

    @pl.loop(0, steps)
    def _(step):
        @pl.loop(0, 2 * UNROLL)
        def _(j):
            entry = ENTRIES + 2 * (2 * UNROLL * step + j)
            first = plan_ref[entry]
            second = plan_ref[entry + 1]
            kind = (first & 1) + 2 * (second & 1)
            at = pl.ds(pl.multiple_of(j * LANES, LANES), LANES)

            @pl.when(kind == 2)
            def _():
                keys[step, :, at] = jnp.where(left_half, tile_of(first), tile_of(second))

            @pl.when(kind == 0)
            def _():
                keys[step, :, at] = jnp.where(left_half, tile_of(first), turned(tile_of(second)))

            @pl.when(kind == 3)
            def _():
                keys[step, :, at] = jnp.where(left_half, turned(tile_of(first)), tile_of(second))

            @pl.when(kind == 1)
            def _():
                keys[step, :, at] = turned(jnp.where(left_half, tile_of(second), tile_of(first)))

        chunk(step).start()

    @pl.loop(0, steps)
    def _(step):
        chunk(step).wait()

    plan_store.wait()


def attention_kernel(
    scale, plan_any, query_any, keys_any, out_ref, plan_ref, plan_sem, query_ref, query_sem, staged, query, scores, top, denom, total, keys_ref, sems
):
    load = pltpu.make_async_copy(query_any, query_ref, query_sem)
    load.start()
    fetch = pltpu.make_async_copy(plan_any.at[pl.ds(0, PLAN)], plan_ref, plan_sem)
    fetch.start()

    def chunk(step):
        return pltpu.make_async_copy(keys_any.at[step], keys_ref.at[step], sems.at[step])

    sources, requests, wide = query_ref.shape
    kv = total.shape[2]
    heads = total.shape[1]
    tiles = kv // LANES
    for step in range(EARLY):
        chunk(step).start()
    fetch.wait()
    used = plan_ref[0]
    steps = (used + 2 * UNROLL - 1) // (2 * UNROLL)

    @pl.loop(EARLY, jnp.maximum(steps, EARLY))
    def _(step):
        chunk(step).start()

    top[...] = jnp.full_like(top, EMPTY)
    denom[...] = jnp.zeros_like(denom)
    total[...] = jnp.zeros_like(total)
    load.wait()
    for t in range(wide // LANES):
        columns = query_ref[:, :, t * LANES : (t + 1) * LANES]
        staged[t] = columns.astype(F32).reshape(sources * requests, LANES)
    for r in range(requests):
        at = pl.ds(r, sources, stride=requests)
        for t in range(tiles):
            columns = slice(t * LANES, (t + 1) * LANES)
            query[r, :sources, columns] = staged[t, at, :].astype(BF16)
            query[r, sources:, columns] = staged[tiles + t, at, :].astype(BF16)
        rows = staged[2 * tiles, at, :].astype(BF16)
        query[r, :sources, kv:] = rows[:, :64]
        query[r, sources:, kv:] = rows[:, 64:]
    lane = lax.broadcasted_iota(jnp.int32, (1, LANES), 1)
    left_half = lane < PAGE
    within = lane & (PAGE - 1)

    def keys(step, u, depth):
        return keys_ref[step, :depth, 2 * LANES * u : 2 * LANES * (u + 1)]

    @pl.loop(0, steps)
    def _(step):
        chunk(step).wait()
        for u in range(UNROLL):
            g = step * UNROLL + u
            owners = [plan_ref[8 + 2 * g + half] for half in range(2)]
            both = jnp.concatenate([query[r] for r in owners], axis=0)
            score = jnp.dot(both, keys(step, u, keys_ref.shape[1]), preferred_element_type=F32)
            for half, r in enumerate(owners):
                rows = jnp.where(
                    left_half,
                    plan_ref[ENTRIES + 4 * g + 2 * half] >> 8,
                    plan_ref[ENTRIES + 4 * g + 2 * half + 1] >> 8,
                )
                part = score[half * heads : (half + 1) * heads, half * LANES : (half + 1) * LANES]
                part = jnp.where(within < rows, part, EMPTY)
                scores[g, :, half * LANES : (half + 1) * LANES] = part
                top[r] = jnp.maximum(top[r], part)

    @pl.loop(jnp.minimum(steps, EARLY), EARLY)
    def _(step):
        chunk(step).wait()

    for r in range(requests):
        top[r] = jnp.broadcast_to(jnp.max(top[r], axis=1, keepdims=True), top.shape[1:])

    @pl.loop(0, steps)
    def _(step):
        for u in range(UNROLL):
            g = step * UNROLL + u
            values = keys(step, u, kv)
            for half in range(2):
                r = plan_ref[8 + 2 * g + half]
                live = jnp.where(2 * g + half < used, 1.0, 0.0)
                part = scores[g, :, half * LANES : (half + 1) * LANES]
                expo = (jnp.exp((part - top[r]) * scale) * live).astype(BF16)
                denom[r] = denom[r] + expo.astype(F32)
                total[r] = total[r] + lax.dot_general(
                    expo,
                    values[:, half * LANES : (half + 1) * LANES],
                    (((1,), (1,)), ((), ())),
                    preferred_element_type=F32,
                )

    for r in range(requests):
        sums = jnp.sum(denom[r], axis=1, keepdims=True)
        some = sums > 0.0
        safe = jnp.where(some, sums, 1.0)
        level = jnp.where(some, top[r][:, :1] * scale + jnp.log(safe), EMPTY)
        rows = total[r] * (1.0 / safe)
        at = pl.ds(r, sources, stride=requests)
        for t in range(tiles):
            columns = slice(t * LANES, (t + 1) * LANES)
            staged[t, at, :] = rows[:sources, columns]
            staged[tiles + t, at, :] = rows[sources:, columns]
        staged[2 * tiles, at, :] = stat_lanes([level[:sources], level[sources:]], sources)
    for t in range(wide // LANES):
        columns = slice(t * LANES, (t + 1) * LANES)
        out_ref[:, :, columns] = staged[t].reshape(sources, requests, LANES).astype(BF16)


def fold_kernel(part_ref, up_any, out_ref, up_ref, sem):
    first = 2 * (lax.axis_index("col") & 1)
    load = pltpu.make_async_copy(up_any.at[pl.ds(first, 2)], up_ref, sem)
    load.start()
    sources, requests, wide = part_ref.shape
    kv = up_ref.shape[1]
    stats = part_ref[:, :, 2 * kv :].astype(F32)
    outputs, levels = [], []
    for j in range(2):
        level = read_stat(stats, j)
        peak = jnp.max(level, axis=0)
        weight = jnp.exp(level - peak[None])
        norm = jnp.sum(weight, axis=0)
        rows = part_ref[:, :, j * kv : (j + 1) * kv].astype(F32)
        rows = jnp.sum(rows * weight, axis=0) / norm
        if j == 0:
            load.wait()
        outputs.append(jnp.dot(rows.astype(BF16), up_ref[j], preferred_element_type=F32))
        levels.append(peak + jnp.log(norm))
    block = jnp.concatenate(outputs + [stat_lanes(levels, requests)], axis=1).astype(BF16)
    for k in range(out_ref.shape[0]):
        out_ref[k] = block


def merge_kernel(part_ref, out_ref):
    width = 2 * LANES
    both = part_ref[...].astype(F32)
    both = both.reshape(both.shape[0] // 2, 2, *both.shape[1:])
    for core in range(2):
        parts = both[:, core]
        stats = parts[:, :, width:]
        for j in range(2):
            level = read_stat(stats, j)
            weight = jnp.exp(level - jnp.max(level, axis=0)[None])
            rows = jnp.sum(parts[:, :, j * LANES : (j + 1) * LANES] * weight, axis=0)
            rows = rows / jnp.sum(weight, axis=0)
            at = (2 * core + j) * LANES
            out_ref[:, at : at + LANES] = rows.astype(BF16)


def vmem():
    return pl.BlockSpec(memory_space=pltpu.VMEM)


def smem():
    return pl.BlockSpec(memory_space=pltpu.SMEM)


def anywhere():
    return pl.BlockSpec(memory_space=pl.ANY)


def params(limit=32 * MIB):
    return pltpu.CompilerParams(vmem_limit_bytes=limit)


def make_queries(nope, rope, key_up, copies):
    requests, heads, width = nope.shape
    kv = key_up.shape[2]
    wide = 2 * kv + 2 * rope.shape[2]
    return pl.pallas_call(
        query_kernel,
        out_shape=jax.ShapeDtypeStruct((copies, requests, wide), BF16),
        in_specs=[anywhere(), anywhere(), anywhere()],
        out_specs=anywhere(),
        scratch_shapes=[
            pltpu.VMEM(nope.shape, BF16),
            pltpu.VMEM(rope.shape, BF16),
            pltpu.VMEM((2, width, kv), BF16),
            pltpu.VMEM((requests, wide), BF16),
            pltpu.SemaphoreType.DMA((3,)),
            pltpu.SemaphoreType.DMA((copies,)),
        ],
        compiler_params=params(ALL_VMEM),
        name="queries",
    )(nope, rope, key_up)


def gather(lengths, table, own, other):
    width, tokens = own.shape
    return pl.pallas_call(
        gather_kernel,
        out_shape=(
            jax.ShapeDtypeStruct((SPREAD,), jnp.int32),
            jax.ShapeDtypeStruct((SPARE + STEPS, width, CHUNK), BF16),
        ),
        in_specs=[smem(), anywhere(), anywhere(), anywhere()],
        out_specs=(anywhere(), anywhere()),
        scratch_shapes=[
            pltpu.SMEM((PLAN,), jnp.int32),
            pltpu.VMEM(table.shape, jnp.int32),
            pltpu.VMEM((2, width, tokens), BF16),
            pltpu.VMEM((STEPS, width, CHUNK), BF16),
            pltpu.VMEM((16, LANES), jnp.int32),
            pltpu.SMEM((16, LANES), jnp.int32),
            pltpu.SMEM((16,), jnp.int32),
            pltpu.SMEM((16,), jnp.int32),
            pltpu.SemaphoreType.DMA,
            pltpu.SemaphoreType.DMA,
            pltpu.SemaphoreType.DMA((2,)),
            pltpu.SemaphoreType.DMA((STEPS,)),
        ],
        compiler_params=params(ALL_VMEM),
        cost_estimate=pl.CostEstimate(
            flops=10_000_000, bytes_accessed=20_000_000, transcendentals=0
        ),
        name="gather",
    )(lengths, table, own, other)


def attend(scale, plan, queries, keys):
    sources, requests, wide = queries.shape
    width = keys.shape[1]
    kv = (wide - 128) // 2
    heads = 2 * sources
    return pl.pallas_call(
        functools.partial(attention_kernel, scale),
        out_shape=jax.ShapeDtypeStruct((sources, requests, wide), BF16),
        in_specs=[anywhere(), anywhere(), anywhere()],
        out_specs=vmem(),
        scratch_shapes=[
            pltpu.SMEM((PLAN,), jnp.int32),
            pltpu.SemaphoreType.DMA,
            pltpu.VMEM(queries.shape, BF16),
            pltpu.SemaphoreType.DMA,
            pltpu.VMEM((wide // LANES, sources * requests, LANES), F32),
            pltpu.VMEM((requests, heads, width), BF16),
            pltpu.VMEM((GROUPS, heads, 2 * LANES), F32),
            pltpu.VMEM((requests, heads, LANES), F32),
            pltpu.VMEM((requests, heads, LANES), F32),
            pltpu.VMEM((requests, heads, kv), F32),
            pltpu.VMEM((STEPS, width, CHUNK), BF16),
            pltpu.SemaphoreType.DMA((STEPS,)),
        ],
        compiler_params=params(40 * MIB),
        cost_estimate=pl.CostEstimate(
            flops=1_200_000_000, bytes_accessed=12_000_000, transcendentals=524_288
        ),
        name="attention",
    )(plan, queries, keys)


def fold(parts, value_up, copies):
    sources, requests, wide = parts.shape
    kv, out = value_up.shape[1:]
    return pl.pallas_call(
        fold_kernel,
        out_shape=jax.ShapeDtypeStruct((copies, requests, 3 * LANES), BF16),
        in_specs=[vmem(), anywhere()],
        out_specs=vmem(),
        scratch_shapes=[pltpu.VMEM((2, kv, out), BF16), pltpu.SemaphoreType.DMA],
        compiler_params=params(),
        name="fold",
    )(parts, value_up)


def merge(parts):
    requests = parts.shape[1]
    return pl.pallas_call(
        merge_kernel,
        out_shape=jax.ShapeDtypeStruct((requests, 4 * LANES), BF16),
        in_specs=[vmem()],
        out_specs=vmem(),
        compiler_params=params(),
        name="merge",
    )(parts)


def local(query_nope, query_rope, key_up, value_up, cache, lengths, table):
    scale = float(query_nope.shape[2] + query_rope.shape[2]) ** -0.5
    rows, cols = lax.axis_size("row"), lax.axis_size("col")
    own = cache.T
    other = lax.ppermute(own, "col", [(i, i ^ 1) for i in range(cols)])
    queries = make_queries(query_nope, query_rope, key_up, rows)
    queries = lax.all_to_all(queries, "row", split_axis=0, concat_axis=0, tiled=True)
    plan, keys = gather(lengths, table, own, other)
    parts = attend(scale, plan, queries, keys)
    parts = lax.all_to_all(parts, "row", split_axis=0, concat_axis=0, tiled=True)
    parts = fold(parts, value_up, cols)
    parts = lax.all_to_all(parts, "col", split_axis=0, concat_axis=0, tiled=True)
    return merge(parts)


def solution(mesh):
    placed = (
        P(None, "row", None),
        P(None, "row", None),
        P("row", None, None),
        P("row", None, None),
        P(("row", "col"), None),
        P(),
        P(),
    )
    return jax.shard_map(
        local, mesh=mesh, in_specs=placed, out_specs=P(None, "row"), check_vma=False
    )
```

```python
import functools

import jax
import jax.numpy as jnp
from jax import lax
from jax.experimental import pallas as pl
from jax.experimental.pallas import tpu as pltpu
from jax.sharding import PartitionSpec as P

PAGE = 64
LANES = 128
EMPTY = -1e30
UNROLL = 4
GROUPS = 40
STEPS = GROUPS // UNROLL
CHUNK = UNROLL * 2 * LANES
MIB = 1024 * 1024
ALL_VMEM = 60 * MIB
ENTRIES = 64
TRASH = 180
PLAN = 1024
EARLY = 3
SPREAD = 6 * 1024 * 1024
F32 = jnp.float32
BF16 = jnp.bfloat16


def three_terms(value):
    high = value.astype(BF16)
    rest = value - high.astype(F32)
    middle = rest.astype(BF16)
    low = (rest - middle.astype(F32)).astype(BF16)
    return high, middle, low


def stat_lanes(values, rows):
    lane = lax.broadcasted_iota(jnp.int32, (rows, LANES), 1)
    out = jnp.zeros((rows, LANES), F32)
    for head, value in enumerate(values):
        for at, term in enumerate(three_terms(value)):
            out = jnp.where(lane == 64 * head + at, term.astype(F32), out)
    return out


def read_stat(lanes, head):
    at = 64 * head
    return lanes[..., at : at + 1] + lanes[..., at + 1 : at + 2] + lanes[..., at + 2 : at + 3]


def query_kernel(nope_any, rope_any, up_ref, out_ref, nope_ref, rope_ref, up, row, sems, out_sems):
    copies, requests, _ = out_ref.shape
    first = 2 * (lax.axis_index("col") & 1)
    loads = [
        pltpu.make_async_copy(nope_any, nope_ref, sems.at[0]),
        pltpu.make_async_copy(rope_any, rope_ref, sems.at[1]),
        pltpu.make_async_copy(up_ref.at[pl.ds(first, 2)], up, sems.at[2]),
    ]
    for load in loads:
        load.start()

    def head_of(ref, j):
        rows = ref[...].astype(F32)
        head = lax.broadcasted_iota(jnp.int32, rows.shape, 1)
        return jnp.sum(jnp.where(head == first + j, rows, 0.0), axis=1).astype(BF16)

    loads[0].wait()
    nopes = [head_of(nope_ref, j) for j in range(2)]
    loads[1].wait()
    ropes = [head_of(rope_ref, j) for j in range(2)]
    loads[2].wait()
    parts = [
        jnp.dot(nopes[j], up[j], preferred_element_type=F32).astype(BF16) for j in range(2)
    ]
    row[...] = jnp.concatenate(parts + ropes, axis=1)
    stores = [
        pltpu.make_async_copy(row, out_ref.at[k], out_sems.at[k]) for k in range(copies)
    ]
    for store in stores:
        store.start()
    for store in stores:
        store.wait()


def gather_kernel(
    length_ref,
    table_any,
    own_ref,
    other_ref,
    plan_any,
    keys_ref,
    plan_ref,
    table_ref,
    cache,
    keys,
    vec,
    sm,
    count,
    fill,
    sem,
    plan_sem,
    cache_sems,
    out_sems,
):
    loads = [
        pltpu.make_async_copy(own_ref, cache.at[0], cache_sems.at[0]),
        pltpu.make_async_copy(other_ref, cache.at[1], cache_sems.at[1]),
    ]
    copy = pltpu.make_async_copy(table_any, table_ref, sem)
    copy.start()
    for load in loads:
        load.start()
    copy.wait()
    column = lax.axis_index("col")
    core = column & 1
    chip = lax.axis_index("row") * (lax.axis_size("col") // 2) + (column >> 1)
    base = chip * 128
    requests, width = table_ref.shape
    page = lax.broadcasted_iota(jnp.int32, (1, width), 1)
    high = lax.broadcasted_iota(jnp.int32, (8, width), 0)
    low = lax.broadcasted_iota(jnp.int32, (16, width), 0)
    total = jnp.zeros((16, 16), F32)
    for r in range(requests):
        slot = table_ref[r : r + 1, :] - base
        live = jnp.clip(length_ref[r] - page * PAGE, 0, PAGE).astype(F32)
        hit = high == (slot >> 4)
        owner = jnp.where(hit, float(r + 1), 0.0)
        rows = jnp.where(hit, live, 0.0)
        left = jnp.concatenate([owner, rows], axis=0).astype(BF16)
        right = jnp.where(low == (slot & 15), 1.0, 0.0).astype(BF16)
        total = total + lax.dot_general(
            left, right, (((1,), (1,)), ((), ())), preferred_element_type=F32
        )
    vec[:, :16] = total.astype(jnp.int32)
    copy = pltpu.make_async_copy(vec, sm, sem)
    copy.start()
    copy.wait()

    def page_of(i, side):
        s = (2 * i + side + PAGE * core) & 127
        return sm[s >> 4, s & 15], sm[8 + (s >> 4), s & 15]

    for r in range(16):
        count[r] = 0

    def page_of(t):
        s = (t + PAGE * core) & 127
        return sm[s >> 4, s & 15], sm[8 + (s >> 4), s & 15]

    @pl.loop(0, 128, unroll=16)
    def _(t):
        owner, _ = page_of(t)
        count[owner] = count[owner] + 1

    start = jnp.int32(0)
    fill[0] = TRASH
    for r in range(requests):
        fill[r + 1] = 4 * start
        groups = (count[r + 1] + 3) >> 2

        @pl.loop(start, start + groups)
        def _(g):
            plan_ref[8 + g] = r
            for at in range(4):
                plan_ref[ENTRIES + 4 * g + at] = 0

        start = start + groups
    plan_ref[0] = start
    for ahead in range(UNROLL - 1):
        plan_ref[8 + start + ahead] = 0
        for at in range(4):
            plan_ref[ENTRIES + 4 * (start + ahead) + at] = 0

    @pl.loop(0, 128, unroll=8)
    def _(t):
        owner, rows = page_of(t)
        at = fill[owner]
        fill[owner] = at + jnp.where(owner > 0, 1, 0)
        plan_ref[ENTRIES + at] = t + (rows << 8)

    plan_store = pltpu.make_async_copy(plan_ref, plan_any.at[pl.ds(0, PLAN)], plan_sem)
    plan_store.start()
    for load in loads:
        load.wait()
    steps = (plan_ref[0] + UNROLL - 1) // UNROLL
    left_half = lax.broadcasted_iota(jnp.int32, (1, LANES), 1) < PAGE

    def tile_of(entry):
        slot = entry & 127
        at = pl.multiple_of(((slot & 63) >> 1) * LANES, LANES)
        return cache[slot >> 6, :, pl.ds(at, LANES)]

    def turned(tile):
        return jnp.concatenate([tile[:, PAGE:], tile[:, :PAGE]], axis=1)

    def chunk(step):
        return pltpu.make_async_copy(keys.at[step], keys_ref.at[step], out_sems.at[step])

    @pl.loop(0, steps)
    def _(step):
        @pl.loop(0, 2 * UNROLL)
        def _(j):
            entry = ENTRIES + 2 * (2 * UNROLL * step + j)
            first = plan_ref[entry]
            second = plan_ref[entry + 1]
            kind = (first & 1) + 2 * (second & 1)
            at = pl.ds(pl.multiple_of(j * LANES, LANES), LANES)

            @pl.when(kind == 2)
            def _():
                keys[step, :, at] = jnp.where(left_half, tile_of(first), tile_of(second))

            @pl.when(kind == 0)
            def _():
                keys[step, :, at] = jnp.where(left_half, tile_of(first), turned(tile_of(second)))

            @pl.when(kind == 3)
            def _():
                keys[step, :, at] = jnp.where(left_half, turned(tile_of(first)), tile_of(second))

            @pl.when(kind == 1)
            def _():
                keys[step, :, at] = turned(jnp.where(left_half, tile_of(second), tile_of(first)))

        chunk(step).start()

    @pl.loop(0, steps)
    def _(step):
        chunk(step).wait()

    plan_store.wait()


def attention_kernel(
    scale, plan_any, query_any, keys_any, out_ref, plan_ref, plan_sem, query_ref, query_sem, staged, query, scores, top, denom, total, keys_ref, sems
):
    load = pltpu.make_async_copy(query_any, query_ref, query_sem)
    load.start()
    fetch = pltpu.make_async_copy(plan_any.at[pl.ds(0, PLAN)], plan_ref, plan_sem)
    fetch.start()

    def chunk(step):
        return pltpu.make_async_copy(keys_any.at[step], keys_ref.at[step], sems.at[step])

    sources, requests, wide = query_ref.shape
    kv = total.shape[2]
    tiles = kv // LANES
    for step in range(EARLY):
        chunk(step).start()
    fetch.wait()
    groups = plan_ref[0]
    steps = (groups + UNROLL - 1) // UNROLL

    @pl.loop(EARLY, jnp.maximum(steps, EARLY))
    def _(step):
        chunk(step).start()

    top[...] = jnp.full_like(top, EMPTY)
    denom[...] = jnp.zeros_like(denom)
    total[...] = jnp.zeros_like(total)
    load.wait()
    for t in range(wide // LANES):
        columns = query_ref[:, :, t * LANES : (t + 1) * LANES]
        staged[t] = columns.astype(F32).reshape(sources * requests, LANES)
    for r in range(requests):
        at = pl.ds(r, sources, stride=requests)
        for t in range(tiles):
            columns = slice(t * LANES, (t + 1) * LANES)
            query[r, :sources, columns] = staged[t, at, :].astype(BF16)
            query[r, sources:, columns] = staged[tiles + t, at, :].astype(BF16)
        rows = staged[2 * tiles, at, :].astype(BF16)
        query[r, :sources, kv:] = rows[:, :64]
        query[r, sources:, kv:] = rows[:, 64:]
    lane = lax.broadcasted_iota(jnp.int32, (1, LANES), 1)
    left_half = lane < PAGE
    within = lane & (PAGE - 1)

    def keys(step, u, depth):
        return keys_ref[step, :depth, 2 * LANES * u : 2 * LANES * (u + 1)]

    whole = (groups + 1) // UNROLL
    left_over = whole * UNROLL < groups

    def score_step(step, count):
        chunk(step).wait()
        for u in range(count):
            g = step * UNROLL + u
            r = plan_ref[8 + g]
            score = jnp.dot(query[r], keys(step, u, keys_ref.shape[1]), preferred_element_type=F32)
            halves = []
            for half in range(2):
                rows = jnp.where(
                    left_half,
                    plan_ref[ENTRIES + 4 * g + 2 * half] >> 8,
                    plan_ref[ENTRIES + 4 * g + 2 * half + 1] >> 8,
                )
                part = score[:, half * LANES : (half + 1) * LANES]
                part = jnp.where(within < rows, part, EMPTY)
                scores[g, :, half * LANES : (half + 1) * LANES] = part
                halves.append(part)
            top[r] = jnp.maximum(top[r], jnp.maximum(*halves))

    @pl.loop(0, whole)
    def _(step):
        score_step(step, UNROLL)

    @pl.when(left_over)
    def _():
        score_step(whole, 2)

    @pl.loop(jnp.minimum(steps, EARLY), EARLY)
    def _(step):
        chunk(step).wait()

    for r in range(requests):
        top[r] = jnp.broadcast_to(jnp.max(top[r], axis=1, keepdims=True), top.shape[1:])

    def value_step(step, count):
        for u in range(count):
            g = step * UNROLL + u
            r = plan_ref[8 + g]
            level = top[r]
            live = jnp.where(g < groups, 1.0, 0.0)
            halves = []
            for half in range(2):
                part = scores[g, :, half * LANES : (half + 1) * LANES]
                halves.append((jnp.exp((part - level) * scale) * live).astype(BF16))
            denom[r] = denom[r] + halves[0].astype(F32) + halves[1].astype(F32)
            total[r] = total[r] + lax.dot_general(
                jnp.concatenate(halves, axis=1),
                keys(step, u, kv),
                (((1,), (1,)), ((), ())),
                preferred_element_type=F32,
            )

    @pl.loop(0, whole)
    def _(step):
        value_step(step, UNROLL)

    @pl.when(left_over)
    def _():
        value_step(whole, 2)

    for r in range(requests):
        sums = jnp.sum(denom[r], axis=1, keepdims=True)
        some = sums > 0.0
        safe = jnp.where(some, sums, 1.0)
        level = jnp.where(some, top[r][:, :1] * scale + jnp.log(safe), EMPTY)
        rows = total[r] * (1.0 / safe)
        at = pl.ds(r, sources, stride=requests)
        for t in range(tiles):
            columns = slice(t * LANES, (t + 1) * LANES)
            staged[t, at, :] = rows[:sources, columns]
            staged[tiles + t, at, :] = rows[sources:, columns]
        staged[2 * tiles, at, :] = stat_lanes([level[:sources], level[sources:]], sources)
    for t in range(wide // LANES):
        columns = slice(t * LANES, (t + 1) * LANES)
        out_ref[:, :, columns] = staged[t].reshape(sources, requests, LANES).astype(BF16)


def fold_kernel(part_ref, up_any, out_ref, up_ref, sem):
    first = 2 * (lax.axis_index("col") & 1)
    load = pltpu.make_async_copy(up_any.at[pl.ds(first, 2)], up_ref, sem)
    load.start()
    sources, requests, wide = part_ref.shape
    kv = up_ref.shape[1]
    stats = part_ref[:, :, 2 * kv :].astype(F32)
    outputs, levels = [], []
    for j in range(2):
        level = read_stat(stats, j)
        peak = jnp.max(level, axis=0)
        weight = jnp.exp(level - peak[None])
        norm = jnp.sum(weight, axis=0)
        rows = part_ref[:, :, j * kv : (j + 1) * kv].astype(F32)
        rows = jnp.sum(rows * weight, axis=0) / norm
        if j == 0:
            load.wait()
        outputs.append(jnp.dot(rows.astype(BF16), up_ref[j], preferred_element_type=F32))
        levels.append(peak + jnp.log(norm))
    block = jnp.concatenate(outputs + [stat_lanes(levels, requests)], axis=1).astype(BF16)
    for k in range(out_ref.shape[0]):
        out_ref[k] = block


def merge_kernel(part_ref, out_ref):
    width = 2 * LANES
    both = part_ref[...].astype(F32)
    both = both.reshape(both.shape[0] // 2, 2, *both.shape[1:])
    for core in range(2):
        parts = both[:, core]
        stats = parts[:, :, width:]
        for j in range(2):
            level = read_stat(stats, j)
            weight = jnp.exp(level - jnp.max(level, axis=0)[None])
            rows = jnp.sum(parts[:, :, j * LANES : (j + 1) * LANES] * weight, axis=0)
            rows = rows / jnp.sum(weight, axis=0)
            at = (2 * core + j) * LANES
            out_ref[:, at : at + LANES] = rows.astype(BF16)


def vmem():
    return pl.BlockSpec(memory_space=pltpu.VMEM)


def smem():
    return pl.BlockSpec(memory_space=pltpu.SMEM)


def anywhere():
    return pl.BlockSpec(memory_space=pl.ANY)


def params(limit=32 * MIB):
    return pltpu.CompilerParams(vmem_limit_bytes=limit)


def make_queries(nope, rope, key_up, copies):
    requests, heads, width = nope.shape
    kv = key_up.shape[2]
    wide = 2 * kv + 2 * rope.shape[2]
    return pl.pallas_call(
        query_kernel,
        out_shape=jax.ShapeDtypeStruct((copies, requests, wide), BF16),
        in_specs=[anywhere(), anywhere(), anywhere()],
        out_specs=anywhere(),
        scratch_shapes=[
            pltpu.VMEM(nope.shape, BF16),
            pltpu.VMEM(rope.shape, BF16),
            pltpu.VMEM((2, width, kv), BF16),
            pltpu.VMEM((requests, wide), BF16),
            pltpu.SemaphoreType.DMA((3,)),
            pltpu.SemaphoreType.DMA((copies,)),
        ],
        compiler_params=params(ALL_VMEM),
        name="queries",
    )(nope, rope, key_up)


def gather(lengths, table, own, other):
    width, tokens = own.shape
    return pl.pallas_call(
        gather_kernel,
        out_shape=(
            jax.ShapeDtypeStruct((SPREAD,), jnp.int32),
            jax.ShapeDtypeStruct((2 * STEPS, width, CHUNK), BF16),
        ),
        in_specs=[smem(), anywhere(), anywhere(), anywhere()],
        out_specs=(anywhere(), anywhere()),
        scratch_shapes=[
            pltpu.SMEM((PLAN,), jnp.int32),
            pltpu.VMEM(table.shape, jnp.int32),
            pltpu.VMEM((2, width, tokens), BF16),
            pltpu.VMEM((STEPS, width, CHUNK), BF16),
            pltpu.VMEM((16, LANES), jnp.int32),
            pltpu.SMEM((16, LANES), jnp.int32),
            pltpu.SMEM((16,), jnp.int32),
            pltpu.SMEM((16,), jnp.int32),
            pltpu.SemaphoreType.DMA,
            pltpu.SemaphoreType.DMA,
            pltpu.SemaphoreType.DMA((2,)),
            pltpu.SemaphoreType.DMA((STEPS,)),
        ],
        compiler_params=params(ALL_VMEM),
        cost_estimate=pl.CostEstimate(
            flops=10_000_000, bytes_accessed=20_000_000, transcendentals=0
        ),
        name="gather",
    )(lengths, table, own, other)


def attend(scale, plan, queries, keys):
    sources, requests, wide = queries.shape
    width = keys.shape[1]
    kv = (wide - 128) // 2
    heads = 2 * sources
    return pl.pallas_call(
        functools.partial(attention_kernel, scale),
        out_shape=jax.ShapeDtypeStruct((sources, requests, wide), BF16),
        in_specs=[anywhere(), anywhere(), anywhere()],
        out_specs=vmem(),
        scratch_shapes=[
            pltpu.SMEM((PLAN,), jnp.int32),
            pltpu.SemaphoreType.DMA,
            pltpu.VMEM(queries.shape, BF16),
            pltpu.SemaphoreType.DMA,
            pltpu.VMEM((wide // LANES, sources * requests, LANES), F32),
            pltpu.VMEM((requests, heads, width), BF16),
            pltpu.VMEM((GROUPS, heads, 2 * LANES), F32),
            pltpu.VMEM((requests, heads, LANES), F32),
            pltpu.VMEM((requests, heads, LANES), F32),
            pltpu.VMEM((requests, heads, kv), F32),
            pltpu.VMEM((STEPS, width, CHUNK), BF16),
            pltpu.SemaphoreType.DMA((STEPS,)),
        ],
        compiler_params=params(40 * MIB),
        cost_estimate=pl.CostEstimate(
            flops=1_200_000_000, bytes_accessed=12_000_000, transcendentals=524_288
        ),
        name="attention",
    )(plan, queries, keys)


def fold(parts, value_up, copies):
    sources, requests, wide = parts.shape
    kv, out = value_up.shape[1:]
    return pl.pallas_call(
        fold_kernel,
        out_shape=jax.ShapeDtypeStruct((copies, requests, 3 * LANES), BF16),
        in_specs=[vmem(), anywhere()],
        out_specs=vmem(),
        scratch_shapes=[pltpu.VMEM((2, kv, out), BF16), pltpu.SemaphoreType.DMA],
        compiler_params=params(),
        name="fold",
    )(parts, value_up)


def merge(parts):
    requests = parts.shape[1]
    return pl.pallas_call(
        merge_kernel,
        out_shape=jax.ShapeDtypeStruct((requests, 4 * LANES), BF16),
        in_specs=[vmem()],
        out_specs=vmem(),
        compiler_params=params(),
        name="merge",
    )(parts)


def local(query_nope, query_rope, key_up, value_up, cache, lengths, table):
    scale = float(query_nope.shape[2] + query_rope.shape[2]) ** -0.5
    rows, cols = lax.axis_size("row"), lax.axis_size("col")
    own = cache.T
    other = lax.ppermute(own, "col", [(i, i ^ 1) for i in range(cols)])
    queries = make_queries(query_nope, query_rope, key_up, rows)
    queries = lax.all_to_all(queries, "row", split_axis=0, concat_axis=0, tiled=True)
    plan, keys = gather(lengths, table, own, other)
    parts = attend(scale, plan, queries, keys)
    parts = lax.all_to_all(parts, "row", split_axis=0, concat_axis=0, tiled=True)
    parts = fold(parts, value_up, cols)
    parts = lax.all_to_all(parts, "col", split_axis=0, concat_axis=0, tiled=True)
    return merge(parts)


def solution(mesh):
    placed = (
        P(None, "row", None),
        P(None, "row", None),
        P("row", None, None),
        P("row", None, None),
        P(("row", "col"), None),
        P(),
        P(),
    )
    return jax.shard_map(
        local, mesh=mesh, in_specs=placed, out_specs=P(None, "row"), check_vma=False
    )
```

```python
import functools

import jax
import jax.numpy as jnp
from jax import lax
from jax.experimental import pallas as pl
from jax.experimental.pallas import tpu as pltpu
from jax.sharding import PartitionSpec as P

PAGE = 64
LANES = 128
EMPTY = -1e30
UNROLL = 4
GROUPS = 40
STEPS = GROUPS // UNROLL
CHUNK = UNROLL * 2 * LANES
MIB = 1024 * 1024
ALL_VMEM = 60 * MIB
ENTRIES = 64
TRASH = 180
PLAN = 1024
EARLY = 3
SPREAD = 6 * 1024 * 1024
F32 = jnp.float32
BF16 = jnp.bfloat16


def three_terms(value):
    high = value.astype(BF16)
    rest = value - high.astype(F32)
    middle = rest.astype(BF16)
    low = (rest - middle.astype(F32)).astype(BF16)
    return high, middle, low


def stat_lanes(values, rows):
    lane = lax.broadcasted_iota(jnp.int32, (rows, LANES), 1)
    out = jnp.zeros((rows, LANES), F32)
    for head, value in enumerate(values):
        for at, term in enumerate(three_terms(value)):
            out = jnp.where(lane == 64 * head + at, term.astype(F32), out)
    return out


def read_stat(lanes, head):
    at = 64 * head
    return lanes[..., at : at + 1] + lanes[..., at + 1 : at + 2] + lanes[..., at + 2 : at + 3]


def query_kernel(nope_any, rope_any, up_ref, out_ref, nope_ref, rope_ref, up, row, sems, out_sems):
    copies, requests, _ = out_ref.shape
    first = 2 * (lax.axis_index("col") & 1)
    loads = [
        pltpu.make_async_copy(nope_any, nope_ref, sems.at[0]),
        pltpu.make_async_copy(rope_any, rope_ref, sems.at[1]),
        pltpu.make_async_copy(up_ref.at[pl.ds(first, 2)], up, sems.at[2]),
    ]
    for load in loads:
        load.start()

    def head_of(ref, j):
        rows = ref[...].astype(F32)
        head = lax.broadcasted_iota(jnp.int32, rows.shape, 1)
        return jnp.sum(jnp.where(head == first + j, rows, 0.0), axis=1).astype(BF16)

    loads[0].wait()
    nopes = [head_of(nope_ref, j) for j in range(2)]
    loads[1].wait()
    ropes = [head_of(rope_ref, j) for j in range(2)]
    loads[2].wait()
    parts = [
        jnp.dot(nopes[j], up[j], preferred_element_type=F32).astype(BF16) for j in range(2)
    ]
    row[...] = jnp.concatenate(parts + ropes, axis=1)
    stores = [
        pltpu.make_async_copy(row, out_ref.at[k], out_sems.at[k]) for k in range(copies)
    ]
    for store in stores:
        store.start()
    for store in stores:
        store.wait()


def gather_kernel(
    length_ref,
    table_any,
    own_ref,
    other_ref,
    plan_any,
    keys_ref,
    plan_ref,
    table_ref,
    cache,
    keys,
    vec,
    sm,
    count,
    fill,
    sem,
    plan_sem,
    cache_sems,
    out_sems,
):
    loads = [
        pltpu.make_async_copy(own_ref, cache.at[0], cache_sems.at[0]),
        pltpu.make_async_copy(other_ref, cache.at[1], cache_sems.at[1]),
    ]
    copy = pltpu.make_async_copy(table_any, table_ref, sem)
    copy.start()
    for load in loads:
        load.start()
    copy.wait()
    column = lax.axis_index("col")
    core = column & 1
    chip = lax.axis_index("row") * (lax.axis_size("col") // 2) + (column >> 1)
    base = chip * 128
    requests, width = table_ref.shape
    page = lax.broadcasted_iota(jnp.int32, (1, width), 1)
    high = lax.broadcasted_iota(jnp.int32, (8, width), 0)
    low = lax.broadcasted_iota(jnp.int32, (16, width), 0)
    total = jnp.zeros((16, 16), F32)
    for r in range(requests):
        slot = table_ref[r : r + 1, :] - base
        live = jnp.clip(length_ref[r] - page * PAGE, 0, PAGE).astype(F32)
        hit = high == (slot >> 4)
        owner = jnp.where(hit, float(r + 1), 0.0)
        rows = jnp.where(hit, live, 0.0)
        left = jnp.concatenate([owner, rows], axis=0).astype(BF16)
        right = jnp.where(low == (slot & 15), 1.0, 0.0).astype(BF16)
        total = total + lax.dot_general(
            left, right, (((1,), (1,)), ((), ())), preferred_element_type=F32
        )
    vec[:, :16] = total.astype(jnp.int32)
    copy = pltpu.make_async_copy(vec, sm, sem)
    copy.start()
    copy.wait()

    def page_of(i, side):
        s = (2 * i + side + PAGE * core) & 127
        return sm[s >> 4, s & 15], sm[8 + (s >> 4), s & 15]

    for r in range(16):
        count[r] = 0

    def page_of(t):
        s = (t + PAGE * core) & 127
        return sm[s >> 4, s & 15], sm[8 + (s >> 4), s & 15]

    @pl.loop(0, 128, unroll=16)
    def _(t):
        owner, _ = page_of(t)
        count[owner] = count[owner] + 1

    start = jnp.int32(0)
    fill[0] = TRASH
    for r in range(requests):
        fill[r + 1] = 4 * start
        groups = (count[r + 1] + 3) >> 2

        @pl.loop(start, start + groups)
        def _(g):
            plan_ref[8 + g] = r
            for at in range(4):
                plan_ref[ENTRIES + 4 * g + at] = 0

        start = start + groups
    plan_ref[0] = start
    for ahead in range(UNROLL - 1):
        plan_ref[8 + start + ahead] = 0
        for at in range(4):
            plan_ref[ENTRIES + 4 * (start + ahead) + at] = 0

    @pl.loop(0, 128, unroll=8)
    def _(t):
        owner, rows = page_of(t)
        at = fill[owner]
        fill[owner] = at + jnp.where(owner > 0, 1, 0)
        plan_ref[ENTRIES + at] = t + (rows << 8)

    plan_store = pltpu.make_async_copy(plan_ref, plan_any.at[pl.ds(0, PLAN)], plan_sem)
    plan_store.start()
    for load in loads:
        load.wait()
    steps = (plan_ref[0] + UNROLL - 1) // UNROLL
    left_half = lax.broadcasted_iota(jnp.int32, (1, LANES), 1) < PAGE

    def tile_of(entry):
        slot = entry & 127
        at = pl.multiple_of(((slot & 63) >> 1) * LANES, LANES)
        return cache[slot >> 6, :, pl.ds(at, LANES)]

    def turned(tile):
        return jnp.concatenate([tile[:, PAGE:], tile[:, :PAGE]], axis=1)

    def chunk(step):
        return pltpu.make_async_copy(keys.at[step], keys_ref.at[step], out_sems.at[step])

    @pl.loop(0, steps)
    def _(step):
        @pl.loop(0, 2 * UNROLL)
        def _(j):
            entry = ENTRIES + 2 * (2 * UNROLL * step + j)
            first = plan_ref[entry]
            second = plan_ref[entry + 1]
            kind = (first & 1) + 2 * (second & 1)
            at = pl.ds(pl.multiple_of(j * LANES, LANES), LANES)

            @pl.when(kind == 2)
            def _():
                keys[step, :, at] = jnp.where(left_half, tile_of(first), tile_of(second))

            @pl.when(kind == 0)
            def _():
                keys[step, :, at] = jnp.where(left_half, tile_of(first), turned(tile_of(second)))

            @pl.when(kind == 3)
            def _():
                keys[step, :, at] = jnp.where(left_half, turned(tile_of(first)), tile_of(second))

            @pl.when(kind == 1)
            def _():
                keys[step, :, at] = turned(jnp.where(left_half, tile_of(second), tile_of(first)))

        chunk(step).start()

    @pl.loop(0, steps)
    def _(step):
        chunk(step).wait()

    plan_store.wait()


def attention_kernel(
    scale, plan_any, query_ref, keys_any, out_ref, plan_ref, plan_sem, staged, query, scores, top, denom, total, keys_ref, sems
):
    fetch = pltpu.make_async_copy(plan_any.at[pl.ds(0, PLAN)], plan_ref, plan_sem)
    fetch.start()

    def chunk(step):
        return pltpu.make_async_copy(keys_any.at[step], keys_ref.at[step], sems.at[step])

    sources, requests, wide = query_ref.shape
    kv = total.shape[2]
    tiles = kv // LANES
    for step in range(EARLY):
        chunk(step).start()
    fetch.wait()
    groups = plan_ref[0]
    steps = (groups + UNROLL - 1) // UNROLL

    @pl.loop(EARLY, jnp.maximum(steps, EARLY))
    def _(step):
        chunk(step).start()

    top[...] = jnp.full_like(top, EMPTY)
    denom[...] = jnp.zeros_like(denom)
    total[...] = jnp.zeros_like(total)
    for t in range(wide // LANES):
        columns = query_ref[:, :, t * LANES : (t + 1) * LANES]
        staged[t] = columns.astype(F32).reshape(sources * requests, LANES)
    for r in range(requests):
        at = pl.ds(r, sources, stride=requests)
        for t in range(tiles):
            columns = slice(t * LANES, (t + 1) * LANES)
            query[r, :sources, columns] = staged[t, at, :].astype(BF16)
            query[r, sources:, columns] = staged[tiles + t, at, :].astype(BF16)
        rows = staged[2 * tiles, at, :].astype(BF16)
        query[r, :sources, kv:] = rows[:, :64]
        query[r, sources:, kv:] = rows[:, 64:]
    lane = lax.broadcasted_iota(jnp.int32, (1, LANES), 1)
    left_half = lane < PAGE
    within = lane & (PAGE - 1)

    def keys(step, u, depth):
        return keys_ref[step, :depth, 2 * LANES * u : 2 * LANES * (u + 1)]

    @pl.loop(0, steps)
    def _(step):
        chunk(step).wait()
        for u in range(UNROLL):
            g = step * UNROLL + u
            r = plan_ref[8 + g]
            score = jnp.dot(query[r], keys(step, u, keys_ref.shape[1]), preferred_element_type=F32)
            halves = []
            for half in range(2):
                rows = jnp.where(
                    left_half,
                    plan_ref[ENTRIES + 4 * g + 2 * half] >> 8,
                    plan_ref[ENTRIES + 4 * g + 2 * half + 1] >> 8,
                )
                part = score[:, half * LANES : (half + 1) * LANES]
                part = jnp.where(within < rows, part, EMPTY)
                scores[g, :, half * LANES : (half + 1) * LANES] = part
                halves.append(part)
            top[r] = jnp.maximum(top[r], jnp.maximum(*halves))

    @pl.loop(jnp.minimum(steps, EARLY), EARLY)
    def _(step):
        chunk(step).wait()

    for r in range(requests):
        top[r] = jnp.broadcast_to(jnp.max(top[r], axis=1, keepdims=True), top.shape[1:])

    @pl.loop(0, steps)
    def _(step):
        for u in range(UNROLL):
            g = step * UNROLL + u
            r = plan_ref[8 + g]
            level = top[r]
            live = jnp.where(g < groups, 1.0, 0.0)
            halves = []
            for half in range(2):
                part = scores[g, :, half * LANES : (half + 1) * LANES]
                halves.append((jnp.exp((part - level) * scale) * live).astype(BF16))
            denom[r] = denom[r] + halves[0].astype(F32) + halves[1].astype(F32)
            total[r] = total[r] + lax.dot_general(
                jnp.concatenate(halves, axis=1),
                keys(step, u, kv),
                (((1,), (1,)), ((), ())),
                preferred_element_type=F32,
            )

    for r in range(requests):
        sums = jnp.sum(denom[r], axis=1, keepdims=True)
        some = sums > 0.0
        safe = jnp.where(some, sums, 1.0)
        level = jnp.where(some, top[r][:, :1] * scale + jnp.log(safe), EMPTY)
        rows = total[r] * (1.0 / safe)
        at = pl.ds(r, sources, stride=requests)
        for t in range(tiles):
            columns = slice(t * LANES, (t + 1) * LANES)
            staged[t, at, :] = rows[:sources, columns]
            staged[tiles + t, at, :] = rows[sources:, columns]
        staged[2 * tiles, at, :] = stat_lanes([level[:sources], level[sources:]], sources)
    for t in range(wide // LANES):
        columns = slice(t * LANES, (t + 1) * LANES)
        out_ref[:, :, columns] = staged[t].reshape(sources, requests, LANES).astype(BF16)


def fold_kernel(part_ref, up_any, out_ref, up_ref, sem):
    first = 2 * (lax.axis_index("col") & 1)
    load = pltpu.make_async_copy(up_any.at[pl.ds(first, 2)], up_ref, sem)
    load.start()
    sources, requests, wide = part_ref.shape
    kv = up_ref.shape[1]
    stats = part_ref[:, :, 2 * kv :].astype(F32)
    outputs, levels = [], []
    for j in range(2):
        level = read_stat(stats, j)
        peak = jnp.max(level, axis=0)
        weight = jnp.exp(level - peak[None])
        norm = jnp.sum(weight, axis=0)
        rows = part_ref[:, :, j * kv : (j + 1) * kv].astype(F32)
        rows = jnp.sum(rows * weight, axis=0) / norm
        if j == 0:
            load.wait()
        outputs.append(jnp.dot(rows.astype(BF16), up_ref[j], preferred_element_type=F32))
        levels.append(peak + jnp.log(norm))
    block = jnp.concatenate(outputs + [stat_lanes(levels, requests)], axis=1).astype(BF16)
    for k in range(out_ref.shape[0]):
        out_ref[k] = block


def merge_kernel(part_ref, out_ref):
    width = 2 * LANES
    both = part_ref[...].astype(F32)
    both = both.reshape(both.shape[0] // 2, 2, *both.shape[1:])
    for core in range(2):
        parts = both[:, core]
        stats = parts[:, :, width:]
        for j in range(2):
            level = read_stat(stats, j)
            weight = jnp.exp(level - jnp.max(level, axis=0)[None])
            rows = jnp.sum(parts[:, :, j * LANES : (j + 1) * LANES] * weight, axis=0)
            rows = rows / jnp.sum(weight, axis=0)
            at = (2 * core + j) * LANES
            out_ref[:, at : at + LANES] = rows.astype(BF16)


def vmem():
    return pl.BlockSpec(memory_space=pltpu.VMEM)


def smem():
    return pl.BlockSpec(memory_space=pltpu.SMEM)


def anywhere():
    return pl.BlockSpec(memory_space=pl.ANY)


def params(limit=32 * MIB):
    return pltpu.CompilerParams(vmem_limit_bytes=limit)


def make_queries(nope, rope, key_up, copies):
    requests, heads, width = nope.shape
    kv = key_up.shape[2]
    wide = 2 * kv + 2 * rope.shape[2]
    return pl.pallas_call(
        query_kernel,
        out_shape=jax.ShapeDtypeStruct((copies, requests, wide), BF16),
        in_specs=[anywhere(), anywhere(), anywhere()],
        out_specs=anywhere(),
        scratch_shapes=[
            pltpu.VMEM(nope.shape, BF16),
            pltpu.VMEM(rope.shape, BF16),
            pltpu.VMEM((2, width, kv), BF16),
            pltpu.VMEM((requests, wide), BF16),
            pltpu.SemaphoreType.DMA((3,)),
            pltpu.SemaphoreType.DMA((copies,)),
        ],
        compiler_params=params(ALL_VMEM),
        name="queries",
    )(nope, rope, key_up)


def gather(lengths, table, own, other):
    width, tokens = own.shape
    return pl.pallas_call(
        gather_kernel,
        out_shape=(
            jax.ShapeDtypeStruct((SPREAD,), jnp.int32),
            jax.ShapeDtypeStruct((2 * STEPS, width, CHUNK), BF16),
        ),
        in_specs=[smem(), anywhere(), anywhere(), anywhere()],
        out_specs=(anywhere(), anywhere()),
        scratch_shapes=[
            pltpu.SMEM((PLAN,), jnp.int32),
            pltpu.VMEM(table.shape, jnp.int32),
            pltpu.VMEM((2, width, tokens), BF16),
            pltpu.VMEM((STEPS, width, CHUNK), BF16),
            pltpu.VMEM((16, LANES), jnp.int32),
            pltpu.SMEM((16, LANES), jnp.int32),
            pltpu.SMEM((16,), jnp.int32),
            pltpu.SMEM((16,), jnp.int32),
            pltpu.SemaphoreType.DMA,
            pltpu.SemaphoreType.DMA,
            pltpu.SemaphoreType.DMA((2,)),
            pltpu.SemaphoreType.DMA((STEPS,)),
        ],
        compiler_params=params(ALL_VMEM),
        cost_estimate=pl.CostEstimate(
            flops=10_000_000, bytes_accessed=20_000_000, transcendentals=0
        ),
        name="gather",
    )(lengths, table, own, other)


def attend(scale, plan, queries, keys):
    sources, requests, wide = queries.shape
    width = keys.shape[1]
    kv = (wide - 128) // 2
    heads = 2 * sources
    return pl.pallas_call(
        functools.partial(attention_kernel, scale),
        out_shape=jax.ShapeDtypeStruct((sources, requests, wide), BF16),
        in_specs=[anywhere(), vmem(), anywhere()],
        out_specs=vmem(),
        scratch_shapes=[
            pltpu.SMEM((PLAN,), jnp.int32),
            pltpu.SemaphoreType.DMA,
            pltpu.VMEM((wide // LANES, sources * requests, LANES), F32),
            pltpu.VMEM((requests, heads, width), BF16),
            pltpu.VMEM((GROUPS, heads, 2 * LANES), F32),
            pltpu.VMEM((requests, heads, LANES), F32),
            pltpu.VMEM((requests, heads, LANES), F32),
            pltpu.VMEM((requests, heads, kv), F32),
            pltpu.VMEM((STEPS, width, CHUNK), BF16),
            pltpu.SemaphoreType.DMA((STEPS,)),
        ],
        compiler_params=params(40 * MIB),
        cost_estimate=pl.CostEstimate(
            flops=1_200_000_000, bytes_accessed=12_000_000, transcendentals=524_288
        ),
        name="attention",
    )(plan, queries, keys)


def fold(parts, value_up, copies):
    sources, requests, wide = parts.shape
    kv, out = value_up.shape[1:]
    return pl.pallas_call(
        fold_kernel,
        out_shape=jax.ShapeDtypeStruct((copies, requests, 3 * LANES), BF16),
        in_specs=[vmem(), anywhere()],
        out_specs=vmem(),
        scratch_shapes=[pltpu.VMEM((2, kv, out), BF16), pltpu.SemaphoreType.DMA],
        compiler_params=params(),
        name="fold",
    )(parts, value_up)


def merge(parts):
    requests = parts.shape[1]
    return pl.pallas_call(
        merge_kernel,
        out_shape=jax.ShapeDtypeStruct((requests, 4 * LANES), BF16),
        in_specs=[vmem()],
        out_specs=vmem(),
        compiler_params=params(),
        name="merge",
    )(parts)


def local(query_nope, query_rope, key_up, value_up, cache, lengths, table):
    scale = float(query_nope.shape[2] + query_rope.shape[2]) ** -0.5
    rows, cols = lax.axis_size("row"), lax.axis_size("col")
    own = cache.T
    other = lax.ppermute(own, "col", [(i, i ^ 1) for i in range(cols)])
    queries = make_queries(query_nope, query_rope, key_up, rows)
    queries = lax.all_to_all(queries, "row", split_axis=0, concat_axis=0, tiled=True)
    plan, keys = gather(lengths, table, own, other)
    parts = attend(scale, plan, queries, keys)
    parts = lax.all_to_all(parts, "row", split_axis=0, concat_axis=0, tiled=True)
    parts = fold(parts, value_up, cols)
    parts = lax.all_to_all(parts, "col", split_axis=0, concat_axis=0, tiled=True)
    return merge(parts)


def solution(mesh):
    placed = (
        P(None, "row", None),
        P(None, "row", None),
        P("row", None, None),
        P("row", None, None),
        P(("row", "col"), None),
        P(),
        P(),
    )
    return jax.shard_map(
        local, mesh=mesh, in_specs=placed, out_specs=P(None, "row"), check_vma=False
    )
```
